512 devices in a mesh: dp: 2 (over y_lo), head: 8 (over z), ctx: 32 (over y_hi, x, core).
Axes of the slice: x: 4, y: 8 (y_hi: 4, y_lo: 2; y = y_hi * 2 + y_lo), z: 8, core: 2. Of those that a mesh axis runs over, the one named last changes fastest.
Arguments:
- queries: bfloat16 [2, 8192, 5120], P('dp', 'ctx', 'head'), may hold values from -1.796875 to 1.796875
- keys: bfloat16 [2, 8192, 5120], P('dp', 'ctx', 'head'), may hold values from -1.796875 to 1.796875
- values: bfloat16 [2, 8192, 5120], P('dp', 'ctx', 'head'), may hold values from -6 to 6
- grad_out: bfloat16 [2, 8192, 5120], P('dp', 'ctx', 'head'), may hold values from -6 to 6
- gain: bfloat16 [5120], P('head'), may hold values from 0.5 to 1.5
- order_flag: int32 [32], P('ctx'), may hold values from 0 to 1
Outputs:
- grad_queries: bfloat16 [2, 8192, 5120], P('dp', 'ctx', 'head')
- grad_keys: bfloat16 [2, 8192, 5120], P('dp', 'ctx', 'head')
- grad_values: bfloat16 [2, 8192, 5120], P('dp', 'ctx', 'head')
- grad_gain: float32 [5120], P('head')
The draws below stay inside these ranges and needn't reach their ends.
All inputs are finite; a program needn't handle non-finite values.
Results may differ from the reference program's by a relative error of at most 0.0014.
Values sent between devices are 32-bit elements; how exact they have to be, the bound alone decides.
A program may use at most 128 MiB of HBM per device.

```python
import jax
import jax.numpy as jnp
from jax import lax

DH = 128
GROUP = 128
HEADS = 40
SEQ = 8192
SEQS = 2
N_CTX = 32


def plant(drawn, key, smallest, largest):
    place = [jax.random.randint(jax.random.fold_in(key, axis), (), 0, length) for axis, length in enumerate(drawn.shape)]
    longest = drawn.shape.index(max(drawn.shape))
    beside = place[:longest] + [(place[longest] + 1) % drawn.shape[longest]] + place[longest + 1:]
    return drawn.at[tuple(place)].set(smallest).at[tuple(beside)].set(largest)


def block_scale(rng, extent, shards, least, largest):
    level, own = 1.0, jax.random.fold_in(rng, 6)
    for axis_at, parts in shards:
        heights = jnp.exp(jax.random.uniform(jax.random.fold_in(own, axis_at), (parts,), jnp.float32, least / len(shards), largest / len(shards)))
        level = level * jnp.repeat(heights, extent[axis_at] // parts).reshape([-1 if axis == axis_at else 1 for axis in range(len(extent))])
    return level


def centred(rng, dims, spread, bound, cuts=(), kind=jnp.bfloat16):
    factor_of = block_scale(rng, dims, cuts, -0.22, 0.18) if cuts else 1.0
    values = jax.random.normal(rng, dims, jnp.float32) * spread * factor_of
    return jnp.minimum(jnp.maximum(values, -bound), bound).astype(kind)


def setup_inputs(seed: int = 0) -> dict:
    seeds = jax.random.split(jax.random.key(seed), 7)
    queries = centred(seeds[0], (SEQS, SEQ, HEADS * DH), 0.3, 1.796875, ((0, 2), (1, 32), (2, 8)))
    keys = centred(seeds[1], (SEQS, SEQ, HEADS * DH), 0.3, 1.796875, ((0, 2), (1, 32), (2, 8)))
    values = centred(seeds[2], (SEQS, SEQ, HEADS * DH), 1.0, 6.0, ((0, 2), (1, 32), (2, 8)))
    grad_out = centred(seeds[3], (SEQS, SEQ, HEADS * DH), 1.0, 6.0, ((0, 2), (1, 32), (2, 8)))
    gain = jnp.clip(1.0 + 0.1 * jax.random.normal(seeds[4], (HEADS * DH,), jnp.float32), 0.5, 1.5).astype(jnp.bfloat16)
    order_flag = plant(jax.random.randint(seeds[5], (N_CTX,), 0, 2), jax.random.fold_in(seeds[5], 1), 0, 1).astype(jnp.int32)
    return {"queries": queries, "keys": keys, "values": values, "grad_out": grad_out, "gain": gain, "order_flag": order_flag}


def contract(form, left, right):
    return jnp.einsum(form, left, right, precision=lax.Precision.HIGHEST)

def seq_index(order_flag):
    pieces = jnp.arange(2 * N_CTX, dtype=jnp.int32)
    device = jnp.where(pieces < N_CTX, pieces, 2 * N_CTX - 1 - pieces).astype(jnp.int32)
    later = (pieces >= N_CTX).astype(jnp.int32)
    slot_id = (later + order_flag[device]) % 2
    starts = device * (2 * GROUP) + slot_id * GROUP
    offsets = jnp.arange(GROUP, dtype=jnp.int32)
    return (starts[:, None] + offsets[None, :]).reshape(-1).astype(jnp.int32)

def to_heads(array, index):
    ordered = jnp.take(array, index, axis=1)
    return ordered.reshape(ordered.shape[0], ordered.shape[1], HEADS, DH).transpose(2, 0, 1, 3)

def blocks(array):
    return array.astype(jnp.float32).reshape(array.shape[0], -1, GROUP, array.shape[-1])

def causal_mask():
    rows_idx = jnp.arange(GROUP, dtype=jnp.int32)[:, None]
    cols_idx = jnp.arange(GROUP, dtype=jnp.int32)[None, :]
    return (rows_idx >= cols_idx).astype(jnp.float32)

def head_forward(items):
    query_b, key_b, value_b = [blocks(item) for item in items]
    kv_state = contract('bnsd,bnse->bnde', key_b, value_b)
    prefix = jnp.cumsum(kv_state, axis=1) - kv_state
    scores = contract('bntd,bnsd->bnts', query_b, key_b) * causal_mask()
    output = contract('bnts,bnse->bnte', scores, value_b) + contract('bntd,bnde->bnte', query_b, prefix)
    return output.reshape(output.shape[0], -1, DH)

def head_backward(items):
    query_b, key_b, value_b, grad_b = [blocks(item) for item in items]
    causal = causal_mask()
    kv_state = contract('bnsd,bnse->bnde', key_b, value_b)
    prefix = jnp.cumsum(kv_state, axis=1) - kv_state
    adjoint = contract('bntd,bnte->bnde', query_b, grad_b)
    suffix = lax.optimization_barrier(jnp.sum(adjoint, axis=1, keepdims=True)) - jnp.cumsum(adjoint, axis=1)
    scores = contract('bntd,bnsd->bnts', query_b, key_b) * causal
    grad_scores = contract('bnte,bnse->bnts', grad_b, value_b) * causal
    grad_q = contract('bnts,bnsd->bntd', grad_scores, key_b) + contract('bnte,bnde->bntd', grad_b, prefix)
    grad_k = contract('bnts,bntd->bnsd', grad_scores, query_b) + contract('bnse,bnde->bnsd', value_b, suffix)
    grad_v = contract('bnts,bnte->bnse', scores, grad_b) + contract('bnsd,bnde->bnse', key_b, suffix)
    shape_out = (grad_b.shape[0], -1, DH)
    return (grad_q.reshape(shape_out).astype(jnp.bfloat16), grad_k.reshape(shape_out).astype(jnp.bfloat16), grad_v.reshape(shape_out).astype(jnp.bfloat16))

def from_heads(array, index):
    flat = array.transpose(1, 2, 0, 3).reshape(array.shape[1], array.shape[2], HEADS * DH)
    return jnp.zeros_like(flat).at[:, index].set(flat)

def reference(queries, keys, values, grad_out, gain, order_flag):
    index = seq_index(order_flag)
    query_h = to_heads(queries, index)
    key_h = to_heads(keys, index)
    value_h = to_heads(values, index)
    grad_h = to_heads(grad_out, index).astype(jnp.float32)
    attn = lax.map(head_forward, (query_h, key_h, value_h))
    gain_h = gain.astype(jnp.float32).reshape(HEADS, 1, 1, DH)
    upstream = grad_h * gain_h
    features = HEADS * DH
    inverse = lax.rsqrt(lax.optimization_barrier(jnp.sum(attn * attn, axis=(0, 3))) / features + 1e-06)
    cross = lax.optimization_barrier(jnp.sum(upstream * attn, axis=(0, 3)))
    grad_attn = upstream * inverse[None, :, :, None] - attn * (cross * inverse ** 3 / features)[None, :, :, None]
    grad_gain = lax.optimization_barrier(jnp.sum(grad_h * attn * inverse[None, :, :, None], axis=(1, 2))).reshape(-1)
    grad_q, grad_k, grad_v = lax.map(head_backward, (query_h, key_h, value_h, grad_attn))
    return (from_heads(grad_q, index), from_heads(grad_k, index), from_heads(grad_v, index), grad_gain)
```

```python
import jax
import jax.numpy as jnp
from jax import lax
from jax.experimental import pallas as pl
from jax.experimental.pallas import tpu as pltpu
from jax.sharding import PartitionSpec as P

MESH = pl.DeviceIdType.MESH
D = 128
NX, NY, NZ = 4, 4, 8
HEADS = 5
PART = D // NX
CHUNKS = ((0, 2), (2, 4), (4, 5))
NC = len(CHUNKS)
F32, BF16 = jnp.float32, jnp.bfloat16


def mm(a, b, ca, cb):
    return lax.dot_general(a, b, (((ca,), (cb,)), ((), ())), preferred_element_type=F32)


def parts(x):
    hi = x.astype(BF16)
    return hi, (x - hi.astype(F32)).astype(BF16)


def wide(*a):
    return jnp.concatenate(a, axis=1)


def tall(*a):
    return jnp.concatenate(a, axis=0)


def kernel(
    flag_ref, gain_ref, q_hbm, k_hbm, v_hbm, g_hbm,
    oq_hbm, ok_hbm, ov_hbm, gg_ref,
    q_ref, k_ref, v_ref, g_ref, oq_ref, ok_ref, ov_ref,
    x_st, y_st, r1, z_st, xr, w_st, yr, base, o_st, t_st, u_st, r2,
    attn, s_hi, s_lo, p_hi, p_lo, a_hi, a_lo, gk_loc, gv_loc,
    sq, cr, inv_b, coef_b, zbuf, gcore, gx, gy, gdp,
    in_sem, out_sem, c1_s, c1_r, x1_s, x1_r, y_s, y_r, x2_s, x2_r, c2_s, c2_r,
    z_s, z_r, gc_s, gc_r, gx_s, gx_r, gy_s, gy_r, gd_s, gd_r,
):
    dp = lax.axis_index("dp")
    z = lax.axis_index("head")
    ctx = lax.axis_index("ctx")
    core = lax.rem(ctx, 2)
    x = lax.rem(ctx // 2, NX)
    y = ctx // (2 * NX)
    sx = jnp.where(core == 0, x, NX - 1 - x)
    sy = jnp.where(core == 0, y, NY - 1 - y)

    def at(yy, xx, cc):
        return {"ctx": (yy * NX + xx) * 2 + cc}

    sibling = at(y, x, 1 - core)
    xs = [lax.rem(x + d, NX) for d in range(1, NX)]
    ys = [lax.rem(y + d, NY) for d in range(1, NY)]
    zs = [lax.rem(z + d, NZ) for d in range(1, NZ)]

    def remote(src, dst, ssem, rsem, device):
        return pltpu.make_async_remote_copy(
            src_ref=src, dst_ref=dst, send_sem=ssem, recv_sem=rsem, device_id=device, device_id_type=MESH
        )

    loads = []
    for i, (src, dst) in enumerate(((k_hbm, k_ref), (v_hbm, v_ref), (q_hbm, q_ref), (g_hbm, g_ref))):
        cp = pltpu.make_async_copy(src, dst, in_sem.at[i])
        cp.start()
        loads.append(cp)

    bar = pltpu.get_barrier_semaphore()
    peers = [sibling] + [at(y, v, core) for v in xs] + [at(v, x, core) for v in ys]
    peers += [{"head": v} for v in zs] + [{"dp": 1 - dp}]
    for p in peers:
        pl.semaphore_signal(bar, inc=1, device_id=p, device_id_type=MESH)

    flag = flag_ref[0]
    first0 = jnp.full((D, D), flag, jnp.int32) == 0
    low = jnp.full((D, D), core, jnp.int32) == 0
    causal = lax.broadcasted_iota(jnp.int32, (D, D), 0) >= lax.broadcasted_iota(jnp.int32, (D, D), 1)
    sends = []

    def cols(h):
        return pl.ds(h * D, D)

    def rows(s):
        return pl.ds(s * D, D)

    def heads(chunk, body):
        for h in range(*chunk):
            body(h)

    def put_state(n, h, s0, s1, mask):
        first = jnp.where(mask, s0, s1)
        both = s0 + s1
        x_st[n, h] = jnp.where(low, first, both)
        y_st[n, h] = jnp.where(low, both, first)

    def stage_core(n, c):
        hs = pl.ds(CHUNKS[c][0], CHUNKS[c][1] - CHUNKS[c][0])
        cp = remote(y_st.at[n, hs], r1.at[n, hs], c1_s.at[n, c], c1_r.at[n, c], sibling)
        cp.start()
        sends.append(cp)
        return cp

    def stage_x(n, c, before):
        hs = pl.ds(CHUNKS[c][0], CHUNKS[c][1] - CHUNKS[c][0])
        before.wait_recv()
        z_st[n, hs] = x_st[n, hs] + r1[n, hs]
        out = []
        for d, xx in enumerate(xs):
            there = pl.multiple_of(xx * PART, PART)
            cp = remote(
                z_st.at[n, hs, pl.ds(there, PART)], xr.at[n, sx, hs], x1_s.at[n, c, d], x1_r.at[n, c, d],
                at(y, xx, core),
            )
            cp.start()
            out.append(cp)
        xr[n, sx, hs] = z_st[n, hs, pl.ds(pl.multiple_of(x * PART, PART), PART)]
        sends.extend(out)
        return out

    def stage_y(n, c, before):
        hs = pl.ds(CHUNKS[c][0], CHUNKS[c][1] - CHUNKS[c][0])
        for cp in before:
            cp.wait_recv()
        w_st[n, hs] = (xr[n, 0, hs] + xr[n, 1, hs]) + (xr[n, 2, hs] + xr[n, 3, hs])
        out = []
        for e in range(1, NY):
            yy = jnp.where(core == 0, lax.rem(y + e, NY), lax.rem(y + NY - e, NY))
            cp = remote(w_st.at[n, hs], yr.at[n, e - 1, hs], y_s.at[n, c, e - 1], y_r.at[n, c, e - 1], at(yy, x, core))

            @pl.when(sy + e < NY)
            def _():
                cp.start()

            out.append(cp)
        return out

    def stage_back(n, c, before):
        hs = pl.ds(CHUNKS[c][0], CHUNKS[c][1] - CHUNKS[c][0])
        base[n, hs] = jnp.zeros_like(base[n, hs])
        for e, cp in enumerate(before, 1):

            @pl.when(sy >= e)
            def _():
                cp.wait_recv()
                base[n, hs] += yr[n, e - 1, hs]

        total = base[n, hs]
        for t in range(NX):
            o_st[n, t, hs] = total
            if t < NX - 1:
                total = total + xr[n, t, hs]
        out = []
        here = pl.ds(pl.multiple_of(x * PART, PART), PART)
        for d, xx in enumerate(xs):
            t = jnp.where(core == 0, xx, NX - 1 - xx)
            cp = remote(o_st.at[n, t, hs], t_st.at[n, hs, here], x2_s.at[n, c, d], x2_r.at[n, c, d], at(y, xx, core))
            cp.start()
            out.append(cp)
        t_st[n, hs, here] = o_st[n, sx, hs]
        sends.extend(out)
        return out

    def stage_swap(n, c, before):
        hs = pl.ds(CHUNKS[c][0], CHUNKS[c][1] - CHUNKS[c][0])
        for cp in before:
            cp.wait_recv()
        u_st[n, hs] = t_st[n, hs] + x_st[n, hs]
        cp = remote(u_st.at[n, hs], r2.at[n, hs], c2_s.at[n, c], c2_r.at[n, c], sibling)
        cp.start()
        sends.append(cp)
        return cp

    def get_states(n, h, mask):
        mine, other = t_st[n, h], r2[n, h]
        own_first = jnp.where(low, x_st[n, h], y_st[n, h])
        first = jnp.where(low, mine, other)
        second = (mine + other) + own_first
        return jnp.where(mask, first, second), jnp.where(mask, second, first)

    loads[0].wait()
    loads[1].wait()
    c1 = []
    for c, chunk in enumerate(CHUNKS):

        def body(h):
            kv = [mm(k_ref[rows(s), cols(h)], v_ref[rows(s), cols(h)], 0, 0) for s in range(2)]
            put_state(0, h, kv[0], kv[1], first0)

        heads(chunk, body)
        if c == 0:
            pl.semaphore_wait(bar, len(peers))
        c1.append(stage_core(0, c))

    def local_attn(h):
        for s in range(2):
            scores = jnp.where(causal, mm(q_ref[rows(s), cols(h)], k_ref[rows(s), cols(h)], 1, 1), 0.0)
            hi, lo = parts(scores)
            s_hi[s, h] = hi
            s_lo[s, h] = lo
            vv = v_ref[rows(s), cols(h)]
            attn[s, h] = mm(wide(hi, lo), tall(vv, vv), 1, 0)

    x1 = [stage_x(0, c, c1[c]) for c in range(NC)]
    loads[2].wait()
    loads[3].wait()
    heads((0, 2), local_attn)
    yy = [stage_y(0, c, x1[c]) for c in range(NC)]
    heads((2, 4), local_attn)
    x2 = [stage_back(0, c, yy[c]) for c in range(NC)]
    heads((4, 5), local_attn)
    c2 = [stage_swap(0, c, x2[c]) for c in range(NC)]

    gain = gain_ref[...].astype(F32)
    for c, chunk in enumerate(CHUNKS):
        c2[c].wait_recv()

        def body(h):
            prefix = get_states(0, h, first0)
            for s in range(2):
                hi, lo = parts(prefix[s])
                p_hi[s, h] = hi
                p_lo[s, h] = lo
                qq = q_ref[rows(s), cols(h)]
                a = attn[s, h] + mm(wide(qq, qq), tall(hi, lo), 1, 0)
                attn[s, h] = a
                up = g_ref[rows(s), cols(h)].astype(F32) * gain[:, h * D : (h + 1) * D]
                if h == 0:
                    sq[s] = a * a
                    cr[s] = up * a
                else:
                    sq[s] += a * a
                    cr[s] += up * a

        heads(chunk, body)

    zero = jnp.zeros((8 - 4, D), F32)
    zbuf[z] = tall(*[jnp.sum(jnp.transpose(m), axis=0, keepdims=True) for m in (sq[0], sq[1], cr[0], cr[1])], zero)
    zc = []
    for d, zz in enumerate(zs):
        cp = remote(zbuf.at[z], zbuf.at[z], z_s.at[d], z_r.at[d], {"head": zz})
        cp.start()
        zc.append(cp)
    sends.extend(zc)
    for cp in zc:
        cp.wait_recv()
    sums = zbuf[0]
    for i in range(1, NZ):
        sums = sums + zbuf[i]
    features = float(HEADS * D * NZ)
    inverse = lax.rsqrt(sums[0:2] * (1.0 / features) + 1e-6)
    coef = sums[2:4] * (inverse * inverse * inverse) * (1.0 / features)
    for s in range(2):
        inv_b[s] = jnp.transpose(jnp.broadcast_to(inverse[s : s + 1], (D, D)))
        coef_b[s] = jnp.transpose(jnp.broadcast_to(coef[s : s + 1], (D, D)))

    last0 = jnp.logical_not(first0)
    c1 = []
    for c, chunk in enumerate(CHUNKS):

        def body(h):
            adj = []
            for s in range(2):
                up = g_ref[rows(s), cols(h)].astype(F32) * gain[:, h * D : (h + 1) * D]
                hi, lo = parts(up * inv_b[s] - attn[s, h] * coef_b[s])
                a_hi[s, h] = hi
                a_lo[s, h] = lo
                qq = q_ref[rows(s), cols(h)]
                adj.append(mm(tall(qq, qq), tall(hi, lo), 0, 0))
            put_state(1, h, adj[0], adj[1], last0)

        heads(chunk, body)
        c1.append(stage_core(1, c))

    def local_grads(h):
        for s in range(2):
            ah, al = a_hi[s, h], a_lo[s, h]
            sh, sl = s_hi[s, h], s_lo[s, h]
            ph, pw = p_hi[s, h], p_lo[s, h]
            qq, kk, vv = (r[rows(s), cols(h)] for r in (q_ref, k_ref, v_ref))
            gs = jnp.where(causal, mm(wide(ah, al), wide(vv, vv), 1, 1), 0.0)
            gh, gl = parts(gs)
            gq = mm(wide(gh, gl), tall(kk, kk), 1, 0) + mm(wide(ah, al, ah), wide(ph, ph, pw), 1, 1)
            oq_ref[rows(s), cols(h)] = gq.astype(BF16)
            gk_loc[s, h] = mm(tall(gh, gl), tall(qq, qq), 0, 0)
            gv_loc[s, h] = mm(tall(sh, sl, sh), tall(ah, ah, al), 0, 0)

    def gain_terms():
        out = []
        for h in range(HEADS):
            terms = [g_ref[rows(s), cols(h)].astype(F32) * attn[s, h] * inv_b[s] for s in range(2)]
            out.append(jnp.sum(terms[0] + terms[1], axis=0, keepdims=True))
        return tall(*out, jnp.zeros((8 - HEADS, D), F32))

    def gain_send(buf, me, ssem, rsem, devices):
        out = []
        for d, device in enumerate(devices):
            cp = remote(buf.at[me], buf.at[me], ssem.at[d], rsem.at[d], device)
            cp.start()
            out.append(cp)
        sends.extend(out)
        return out

    def gain_sum(buf, count, copies):
        for cp in copies:
            cp.wait_recv()
        total = buf[0]
        for i in range(1, count):
            total = total + buf[i]
        return total

    x1 = [stage_x(1, c, c1[c]) for c in range(NC)]
    gcore[core] = gain_terms()
    gc = gain_send(gcore, core, gc_s, gc_r, [sibling])
    heads((0, 2), local_grads)
    yy = [stage_y(1, c, x1[c]) for c in range(NC)]
    gx[x] = gain_sum(gcore, 2, gc)
    gc = gain_send(gx, x, gx_s, gx_r, [at(y, v, core) for v in xs])
    heads((2, 4), local_grads)
    x2 = [stage_back(1, c, yy[c]) for c in range(NC)]
    gy[y] = gain_sum(gx, NX, gc)
    gc = gain_send(gy, y, gy_s, gy_r, [at(v, x, core) for v in ys])
    heads((4, 5), local_grads)
    store_q = pltpu.make_async_copy(oq_ref, oq_hbm, out_sem.at[0])
    store_q.start()
    c2 = [stage_swap(1, c, x2[c]) for c in range(NC)]
    gdp[dp] = gain_sum(gy, NY, gc)
    gc = gain_send(gdp, dp, gd_s, gd_r, [{"dp": 1 - dp}])

    for c, chunk in enumerate(CHUNKS):
        c2[c].wait_recv()

        def body(h):
            suffix = get_states(1, h, last0)
            for s in range(2):
                hi, lo = parts(suffix[s])
                kk, vv = (r[rows(s), cols(h)] for r in (k_ref, v_ref))
                gk = gk_loc[s, h] + mm(wide(vv, vv), wide(hi, lo), 1, 1)
                gv = gv_loc[s, h] + mm(wide(kk, kk), tall(hi, lo), 1, 0)
                ok_ref[rows(s), cols(h)] = gk.astype(BF16)
                ov_ref[rows(s), cols(h)] = gv.astype(BF16)

        heads(chunk, body)
    store_k = pltpu.make_async_copy(ok_ref, ok_hbm, out_sem.at[1])
    store_v = pltpu.make_async_copy(ov_ref, ov_hbm, out_sem.at[2])
    store_k.start()
    store_v.start()
    gg_ref[...] = gain_sum(gdp, 2, gc)

    for cp in sends:
        cp.wait_send()
    for n in range(2):
        for c, chunk in enumerate(CHUNKS):
            hs = pl.ds(chunk[0], chunk[1] - chunk[0])
            for e in range(1, NY):

                @pl.when(sy + e < NY)
                def _():
                    remote(
                        w_st.at[n, hs], yr.at[n, e - 1, hs], y_s.at[n, c, e - 1], y_r.at[n, c, e - 1], sibling
                    ).wait_send()

    store_q.wait()
    store_k.wait()
    store_v.wait()


def shards(queries, keys, values, grad_out, gain, order_flag):
    shape = queries.shape
    tokens, width = shape[1], shape[2]
    flat = [a.reshape(tokens, width) for a in (queries, keys, values, grad_out)]
    state = (2, HEADS, D, D)
    piece = (HEADS, PART, D)
    dma = pltpu.SemaphoreType.DMA
    scratch = [pltpu.VMEM((tokens, width), BF16)] * 7
    scratch += [pltpu.VMEM(state, F32)] * 4
    scratch += [
        pltpu.VMEM((2, NX) + piece, F32),
        pltpu.VMEM((2,) + piece, F32),
        pltpu.VMEM((2, NY - 1) + piece, F32),
        pltpu.VMEM((2,) + piece, F32),
        pltpu.VMEM((2, NX) + piece, F32),
    ]
    scratch += [pltpu.VMEM(state, F32)] * 3
    scratch += [pltpu.VMEM(state, F32)]
    scratch += [pltpu.VMEM(state, BF16)] * 6
    scratch += [pltpu.VMEM(state, F32)] * 2
    scratch += [pltpu.VMEM((2, D, D), F32)] * 4
    scratch += [pltpu.VMEM((n, 8, D), F32) for n in (NZ, 2, NX, NY, 2)]
    scratch += [dma((4,)), dma((3,))]
    for shape_of in ((2, NC), (2, NC, NX - 1), (2, NC, NY - 1), (2, NC, NX - 1), (2, NC)):
        scratch += [dma(shape_of)] * 2
    for count in (NZ - 1, 1, NX - 1, NY - 1, 1):
        scratch += [dma((count,))] * 2
    hbm = pl.BlockSpec(memory_space=pl.ANY)
    vmem = pl.BlockSpec(memory_space=pltpu.VMEM)
    out = jax.ShapeDtypeStruct((tokens, width), BF16)
    gq, gk, gv, gg = pl.pallas_call(
        kernel,
        name="layer_backward",
        out_shape=(out, out, out, jax.ShapeDtypeStruct((8, D), F32)),
        in_specs=[pl.BlockSpec(memory_space=pltpu.SMEM), vmem, hbm, hbm, hbm, hbm],
        out_specs=(hbm, hbm, hbm, vmem),
        scratch_shapes=scratch,
        compiler_params=pltpu.CompilerParams(
            collective_id=0, has_side_effects=True, vmem_limit_bytes=48 * 1024 * 1024
        ),
    )(order_flag, gain.reshape(1, width), *flat)
    return gq.reshape(shape), gk.reshape(shape), gv.reshape(shape), gg[:HEADS].reshape(width)


def solution(mesh):
    rows = P("dp", "ctx", "head")
    return jax.shard_map(
        shards,
        mesh=mesh,
        in_specs=(rows, rows, rows, rows, P("head"), P("ctx")),
        out_specs=(rows, rows, rows, P("head")),
        check_vma=False,
    )
```

```python
import jax
import jax.numpy as jnp
from jax import lax
from jax.experimental import pallas as pl
from jax.experimental.pallas import tpu as pltpu
from jax.sharding import PartitionSpec as P

MESH = pl.DeviceIdType.MESH
D = 128
NX, NY, NZ = 4, 4, 8
HEADS = 5
PART = D // NX
CHUNKS = tuple((h, h + 1) for h in range(HEADS))
NC = len(CHUNKS)
PIECES = 1
F32, BF16 = jnp.float32, jnp.bfloat16


def mm(a, b, ca, cb):
    return lax.dot_general(a, b, (((ca,), (cb,)), ((), ())), preferred_element_type=F32)


def parts(x):
    hi = x.astype(BF16)
    return hi, (x - hi.astype(F32)).astype(BF16)


def wide(*a):
    return jnp.concatenate(a, axis=1)


def tall(*a):
    return jnp.concatenate(a, axis=0)


def kernel(
    flag_ref, gain_hbm, q_hbm, k_hbm, v_hbm, g_hbm,
    oq_ref, ok_ref, ov_ref, gg_ref,
    q_ref, k_ref, v_ref, g_ref, gain_ref,
    x_st, y_st, r1, z_st, xr, w_st, yr, base, o_st, t_st, u_st, r2,
    attn, s_hi, s_lo, p_hi, p_lo, a_hi, a_lo, qt, up, gk_loc, gv_loc,
    sq, cr, inv_b, coef_b, zbuf, gcore, gx, gy, gdp,
    in_sem, kv_sem, c1_s, c1_r, x1_s, x1_r, y_s, y_r, x2_s, x2_r, c2_s, c2_r,
    z_s, z_r, gc_s, gc_r, gx_s, gx_r, gy_s, gy_r, gd_s, gd_r,
):
    dp = lax.axis_index("dp")
    z = lax.axis_index("head")
    ctx = lax.axis_index("ctx")
    core = lax.rem(ctx, 2)
    x = lax.rem(ctx // 2, NX)
    y = ctx // (2 * NX)
    sx = jnp.where(core == 0, x, NX - 1 - x)
    sy = jnp.where(core == 0, y, NY - 1 - y)

    def at(yy, xx, cc):
        return {"ctx": (yy * NX + xx) * 2 + cc}

    sibling = at(y, x, 1 - core)
    xs = [lax.rem(x + d, NX) for d in (2, 1, 3)]
    ys = [lax.rem(y + d, NY) for d in range(1, NY)]
    zs = [lax.rem(z + d, NZ) for d in range(1, NZ)]

    def remote(src, dst, ssem, rsem, device):
        return pltpu.make_async_remote_copy(
            src_ref=src, dst_ref=dst, send_sem=ssem, recv_sem=rsem, device_id=device, device_id_type=MESH
        )

    def load(src, dst, sem):
        cp = pltpu.make_async_copy(src, dst, sem)
        cp.start()
        return cp

    def load_head(h):
        where = (slice(None), pl.ds(h * D, D))
        return [load(src.at[where], dst.at[where], kv_sem.at[i, h]) for i, (src, dst) in enumerate(((k_hbm, k_ref), (v_hbm, v_ref)))]

    kv_loads = [load_head(0)]
    bar = pltpu.get_barrier_semaphore()
    peers = [sibling] + [at(y, v, core) for v in xs] + [at(v, x, core) for v in ys]
    peers += [{"head": v} for v in zs] + [{"dp": 1 - dp}]
    for p in peers:
        pl.semaphore_signal(bar, inc=1, device_id=p, device_id_type=MESH)
    kv_loads += [load_head(h) for h in range(1, HEADS)]
    loads = [load(*c, in_sem.at[i]) for i, c in enumerate(((q_hbm, q_ref), (g_hbm, g_ref), (gain_hbm, gain_ref)))]

    flag = flag_ref[0]
    first0 = jnp.full((D, D), flag, jnp.int32) == 0
    low = jnp.full((D, D), core, jnp.int32) == 0
    causal = lax.broadcasted_iota(jnp.int32, (D, D), 0) >= lax.broadcasted_iota(jnp.int32, (D, D), 1)
    sends = []

    def cols(h):
        return pl.ds(h * D, D)

    def rows(s):
        return pl.ds(s * D, D)

    def heads(chunk, body):
        for h in range(*chunk):
            body(h)

    def put_state(n, h, s0, s1, mask):
        first = jnp.where(mask, s0, s1)
        both = s0 + s1
        x_st[n, h] = jnp.where(low, first, both)
        y_st[n, h] = jnp.where(low, both, first)

    def stage_core(n, c):
        hs = pl.ds(CHUNKS[c][0], CHUNKS[c][1] - CHUNKS[c][0])
        cp = remote(y_st.at[n, hs], r1.at[n, hs], c1_s.at[n, c], c1_r.at[n, c], sibling)
        cp.start()
        sends.append(cp)
        return cp

    def stage_x(n, c, before):
        hs = pl.ds(CHUNKS[c][0], CHUNKS[c][1] - CHUNKS[c][0])
        before.wait_recv()
        z_st[n, hs] = x_st[n, hs] + r1[n, hs]
        out = []
        for d, xx in enumerate(xs):
            there = pl.multiple_of(xx * PART, PART)
            cp = remote(
                z_st.at[n, hs, pl.ds(there, PART)], xr.at[n, sx, hs], x1_s.at[n, c, d], x1_r.at[n, c, d],
                at(y, xx, core),
            )
            cp.start()
            out.append(cp)
        xr[n, sx, hs] = z_st[n, hs, pl.ds(pl.multiple_of(x * PART, PART), PART)]
        sends.extend(out)
        return out

    def stage_y(n, c, before):
        hs = pl.ds(CHUNKS[c][0], CHUNKS[c][1] - CHUNKS[c][0])
        for cp in before:
            cp.wait_recv()
        w_st[n, hs] = (xr[n, 0, hs] + xr[n, 1, hs]) + (xr[n, 2, hs] + xr[n, 3, hs])
        out = []
        for e in (2, 1, 3):
            yy = jnp.where(core == 0, lax.rem(y + e, NY), lax.rem(y + NY - e, NY))
            cp = remote(w_st.at[n, hs], yr.at[n, e - 1, hs], y_s.at[n, c, e - 1], y_r.at[n, c, e - 1], at(yy, x, core))

            @pl.when(sy + e < NY)
            def _():
                cp.start()

            out.append(cp)
        return [out[1], out[0], out[2]]

    def stage_back(n, c, before):
        hs = pl.ds(CHUNKS[c][0], CHUNKS[c][1] - CHUNKS[c][0])
        base[n, hs] = jnp.zeros_like(base[n, hs])
        for e, cp in enumerate(before, 1):

            @pl.when(sy >= e)
            def _():
                cp.wait_recv()
                base[n, hs] += yr[n, e - 1, hs]

        total = base[n, hs]
        for t in range(NX):
            o_st[n, t, hs] = total
            if t < NX - 1:
                total = total + xr[n, t, hs]
        out = []
        here = pl.ds(pl.multiple_of(x * PART, PART), PART)
        for d, xx in enumerate(xs):
            t = jnp.where(core == 0, xx, NX - 1 - xx)
            cp = remote(o_st.at[n, t, hs], t_st.at[n, hs, here], x2_s.at[n, c, d], x2_r.at[n, c, d], at(y, xx, core))
            cp.start()
            out.append(cp)
        t_st[n, hs, here] = o_st[n, sx, hs]
        sends.extend(out)
        return out

    def stage_swap(n, c, before):
        hs = pl.ds(CHUNKS[c][0], CHUNKS[c][1] - CHUNKS[c][0])
        for cp in before:
            cp.wait_recv()
        u_st[n, hs] = t_st[n, hs] + x_st[n, hs]
        cp = remote(u_st.at[n, hs], r2.at[n, hs], c2_s.at[n, c], c2_r.at[n, c], sibling)
        cp.start()
        sends.append(cp)
        return cp

    def get_states(n, h, mask):
        mine, other = t_st[n, h], r2[n, h]
        own_first = jnp.where(low, x_st[n, h], y_st[n, h])
        first = jnp.where(low, mine, other)
        second = (mine + other) + own_first
        return jnp.where(mask, first, second), jnp.where(mask, second, first)

    c1 = []
    for c, chunk in enumerate(CHUNKS):

        def body(h):
            for cp in kv_loads[h]:
                cp.wait()
            kv = [mm(k_ref[rows(s), cols(h)], v_ref[rows(s), cols(h)], 0, 0) for s in range(2)]
            put_state(0, h, kv[0], kv[1], first0)

        heads(chunk, body)
        if c == 0:
            pl.semaphore_wait(bar, len(peers))
        c1.append(stage_core(0, c))

    def local_attn(h):
        for s in range(2):
            qt[s, h] = jnp.transpose(q_ref[rows(s), cols(h)])
            up[s, h] = g_ref[rows(s), cols(h)].astype(F32) * gain[:, h * D : (h + 1) * D]
            scores = jnp.where(causal, mm(q_ref[rows(s), cols(h)], k_ref[rows(s), cols(h)], 1, 1), 0.0)
            hi, lo = parts(scores)
            s_hi[s, h] = hi
            s_lo[s, h] = lo
            vv = v_ref[rows(s), cols(h)]
            attn[s, h] = mm(wide(hi, lo), tall(vv, vv), 1, 0)

    x1 = [stage_x(0, c, c1[c]) for c in range(NC)]
    for cp in loads:
        cp.wait()
    gain = gain_ref[...].astype(F32).reshape(1, HEADS * D)
    heads((0, 2), local_attn)
    yy = [stage_y(0, c, x1[c]) for c in range(NC)]
    heads((2, 5), local_attn)
    x2 = [stage_back(0, c, yy[c]) for c in range(NC)]
    c2 = [stage_swap(0, c, x2[c]) for c in range(NC)]

    for c, chunk in enumerate(CHUNKS):
        c2[c].wait_recv()

        def body(h):
            prefix = get_states(0, h, first0)
            for s in range(2):
                hi, lo = parts(prefix[s])
                p_hi[s, h] = hi
                p_lo[s, h] = lo
                qq = q_ref[rows(s), cols(h)]
                a = attn[s, h] + mm(wide(qq, qq), tall(hi, lo), 1, 0)
                attn[s, h] = a
                if h == 0:
                    sq[s] = a * a
                    cr[s] = up[s, h] * a
                else:
                    sq[s] += a * a
                    cr[s] += up[s, h] * a

        heads(chunk, body)

    zero = jnp.zeros((8 - 4, D), F32)
    zbuf[z] = tall(*[jnp.sum(jnp.transpose(m), axis=0, keepdims=True) for m in (sq[0], sq[1], cr[0], cr[1])], zero)
    zc = []
    for d, zz in enumerate(zs):
        cp = remote(zbuf.at[z], zbuf.at[z], z_s.at[d], z_r.at[d], {"head": zz})
        cp.start()
        zc.append(cp)
    sends.extend(zc)
    for cp in zc:
        cp.wait_recv()
    sums = zbuf[0]
    for i in range(1, NZ):
        sums = sums + zbuf[i]
    features = float(HEADS * D * NZ)
    inverse = lax.rsqrt(sums[0:2] * (1.0 / features) + 1e-6)
    coef = sums[2:4] * (inverse * inverse * inverse) * (1.0 / features)
    for s in range(2):
        inv_b[s] = jnp.transpose(jnp.broadcast_to(inverse[s : s + 1], (D, D)))
        coef_b[s] = jnp.transpose(jnp.broadcast_to(coef[s : s + 1], (D, D)))

    last0 = jnp.logical_not(first0)
    c1 = []
    for c, chunk in enumerate(CHUNKS):

        def body(h):
            adj = []
            for s in range(2):
                hi, lo = parts(up[s, h] * inv_b[s] - attn[s, h] * coef_b[s])
                a_hi[s, h] = hi
                a_lo[s, h] = lo
                qq = qt[s, h]
                adj.append(mm(wide(qq, qq), tall(hi, lo), 1, 0))
            put_state(1, h, adj[0], adj[1], last0)

        heads(chunk, body)
        c1.append(stage_core(1, c))

    def local_grads(h):
        for s in range(2):
            ah, al = a_hi[s, h], a_lo[s, h]
            sh, sl = s_hi[s, h], s_lo[s, h]
            ph, pw = p_hi[s, h], p_lo[s, h]
            qq, kk, vv = (r[rows(s), cols(h)] for r in (q_ref, k_ref, v_ref))
            gs = jnp.where(causal, mm(wide(ah, al), wide(vv, vv), 1, 1), 0.0)
            gh, gl = parts(gs)
            gq = mm(wide(gh, gl), tall(kk, kk), 1, 0) + mm(wide(ah, al, ah), wide(ph, ph, pw), 1, 1)
            oq_ref[rows(s), cols(h)] = gq.astype(BF16)
            gk_loc[s, h] = mm(tall(gh, gl), tall(qq, qq), 0, 0)
            gv_loc[s, h] = mm(tall(sh, sl, sh), tall(ah, ah, al), 0, 0)

    def gain_terms():
        out = []
        for h in range(HEADS):
            terms = [g_ref[rows(s), cols(h)].astype(F32) * attn[s, h] * inv_b[s] for s in range(2)]
            out.append(jnp.sum(terms[0] + terms[1], axis=0, keepdims=True))
        return tall(*out, jnp.zeros((8 - HEADS, D), F32))

    def gain_send(buf, me, ssem, rsem, devices):
        out = []
        for d, device in enumerate(devices):
            cp = remote(buf.at[me], buf.at[me], ssem.at[d], rsem.at[d], device)
            cp.start()
            out.append(cp)
        sends.extend(out)
        return out

    def gain_sum(buf, count, copies):
        for cp in copies:
            cp.wait_recv()
        total = buf[0]
        for i in range(1, count):
            total = total + buf[i]
        return total

    x1 = [stage_x(1, c, c1[c]) for c in range(NC)]
    gcore[core] = gain_terms()
    gc = gain_send(gcore, core, gc_s, gc_r, [sibling])
    heads((0, 2), local_grads)
    yy = [stage_y(1, c, x1[c]) for c in range(NC)]
    gx[x] = gain_sum(gcore, 2, gc)
    gc = gain_send(gx, x, gx_s, gx_r, [at(y, v, core) for v in xs])
    heads((2, 4), local_grads)
    x2 = [stage_back(1, c, yy[c]) for c in range(NC)]
    gy[y] = gain_sum(gx, NX, gc)
    gc = gain_send(gy, y, gy_s, gy_r, [at(v, x, core) for v in ys])
    heads((4, 5), local_grads)
    c2 = [stage_swap(1, c, x2[c]) for c in range(NC)]
    gdp[dp] = gain_sum(gy, NY, gc)
    gc = gain_send(gdp, dp, gd_s, gd_r, [{"dp": 1 - dp}])

    for c, chunk in enumerate(CHUNKS):
        c2[c].wait_recv()

        def body(h):
            suffix = get_states(1, h, last0)
            for s in range(2):
                hi, lo = parts(suffix[s])
                kk, vv = (r[rows(s), cols(h)] for r in (k_ref, v_ref))
                gk = gk_loc[s, h] + mm(wide(vv, vv), wide(hi, lo), 1, 1)
                gv = gv_loc[s, h] + mm(wide(kk, kk), tall(hi, lo), 1, 0)
                ok_ref[rows(s), cols(h)] = gk.astype(BF16)
                ov_ref[rows(s), cols(h)] = gv.astype(BF16)

        heads(chunk, body)
    gg_ref[...] = gain_sum(gdp, 2, gc)

    for cp in sends:
        cp.wait_send()
    for n in range(2):
        for c, chunk in enumerate(CHUNKS):
            hs = pl.ds(chunk[0], chunk[1] - chunk[0])
            for e in range(1, NY):

                @pl.when(sy + e < NY)
                def _():
                    remote(
                        w_st.at[n, hs], yr.at[n, e - 1, hs], y_s.at[n, c, e - 1], y_r.at[n, c, e - 1], sibling
                    ).wait_send()


def write_kernel(gq, gk, gv, gg, oq, ok, ov, og, sem):
    copies = []
    for i, (src, dst) in enumerate(((gq, oq), (gk, ok), (gv, ov))):
        for j in range(PIECES):
            rows = pl.ds(j * (src.shape[0] // PIECES), src.shape[0] // PIECES)
            copies.append(pltpu.make_async_copy(src.at[rows], dst.at[rows], sem.at[i, j]))
            copies[-1].start()
    for h in range(HEADS):
        og[pl.ds(h * D, D)] = gg[h]
    for cp in copies:
        cp.wait()


def shards(queries, keys, values, grad_out, gain, order_flag):
    shape = queries.shape
    tokens, width = shape[1], shape[2]
    flat = [a.reshape(tokens, width) for a in (queries, keys, values, grad_out)]
    gain = pltpu.with_memory_space_constraint(gain, pltpu.HBM)
    state = (2, HEADS, D, D)
    piece = (HEADS, PART, D)
    dma = pltpu.SemaphoreType.DMA
    scratch = [pltpu.VMEM((tokens, width), BF16)] * 4 + [pltpu.VMEM((width,), BF16)]
    scratch += [pltpu.VMEM(state, F32)] * 4
    scratch += [
        pltpu.VMEM((2, NX) + piece, F32),
        pltpu.VMEM((2,) + piece, F32),
        pltpu.VMEM((2, NY - 1) + piece, F32),
        pltpu.VMEM((2,) + piece, F32),
        pltpu.VMEM((2, NX) + piece, F32),
    ]
    scratch += [pltpu.VMEM(state, F32)] * 3
    scratch += [pltpu.VMEM(state, F32)]
    scratch += [pltpu.VMEM(state, BF16)] * 7
    scratch += [pltpu.VMEM(state, F32)] * 3
    scratch += [pltpu.VMEM((2, D, D), F32)] * 4
    scratch += [pltpu.VMEM((n, 8, D), F32) for n in (NZ, 2, NX, NY, 2)]
    scratch += [dma((3,)), dma((2, HEADS))]
    for shape_of in ((2, NC), (2, NC, NX - 1), (2, NC, NY - 1), (2, NC, NX - 1), (2, NC)):
        scratch += [dma(shape_of)] * 2
    for count in (NZ - 1, 1, NX - 1, NY - 1, 1):
        scratch += [dma((count,))] * 2
    hbm = pl.BlockSpec(memory_space=pl.ANY)
    vmem = pl.BlockSpec(memory_space=pltpu.VMEM)
    out = jax.ShapeDtypeStruct((tokens, width), BF16)
    inner = pltpu.VMEM((tokens, width), BF16)
    flat = [pltpu.with_memory_space_constraint(a, pltpu.HBM) for a in flat]
    gq, gk, gv, gg = pl.pallas_call(
        kernel,
        name="layer_backward",
        out_shape=(inner, inner, inner, jax.ShapeDtypeStruct((8, D), F32)),
        in_specs=[pl.BlockSpec(memory_space=pltpu.SMEM), hbm, hbm, hbm, hbm, hbm],
        out_specs=(vmem, vmem, vmem, vmem),
        scratch_shapes=scratch,
        compiler_params=pltpu.CompilerParams(
            collective_id=0, has_side_effects=True, vmem_limit_bytes=32 * 1024 * 1024
        ),
    )(order_flag, gain, *flat)
    gq, gk, gv = [pltpu.with_memory_space_constraint(a, pltpu.VMEM) for a in (gq, gk, gv)]
    gq, gk, gv, gg = pl.pallas_call(
        write_kernel,
        name="write_results",
        out_shape=(out, out, out, jax.ShapeDtypeStruct((width,), F32)),
        in_specs=[vmem, vmem, vmem, vmem],
        out_specs=(hbm, hbm, hbm, vmem),
        scratch_shapes=[dma((3, PIECES))],
        compiler_params=pltpu.CompilerParams(vmem_limit_bytes=32 * 1024 * 1024),
    )(gq, gk, gv, gg)
    return gq.reshape(shape), gk.reshape(shape), gv.reshape(shape), gg


def solution(mesh):
    rows = P("dp", "ctx", "head")
    return jax.shard_map(
        shards,
        mesh=mesh,
        in_specs=(rows, rows, rows, rows, P("head"), P("ctx")),
        out_specs=(rows, rows, rows, P("head")),
        check_vma=False,
    )
```

```python
import jax
import jax.numpy as jnp
from jax import lax
from jax.experimental import pallas as pl
from jax.experimental.pallas import tpu as pltpu
from jax.sharding import PartitionSpec as P

MESH = pl.DeviceIdType.MESH
D = 128
NX, NY, NZ = 4, 4, 8
HEADS = 5
PART = D // NX
CHUNKS = tuple((h, h + 1) for h in range(HEADS))
NC = len(CHUNKS)
PIECES = 1
STRAIGHT = (0,)
F32, BF16 = jnp.float32, jnp.bfloat16


def mm(a, b, ca, cb):
    return lax.dot_general(a, b, (((ca,), (cb,)), ((), ())), preferred_element_type=F32)


def parts(x):
    hi = x.astype(BF16)
    return hi, (x - hi.astype(F32)).astype(BF16)


def wide(*a):
    return jnp.concatenate(a, axis=1)


def tall(*a):
    return jnp.concatenate(a, axis=0)


def kernel(
    flag_ref, gain_hbm, q_hbm, k_hbm, v_hbm, g_hbm,
    oq_ref, ok_ref, ov_ref, gg_ref,
    q_ref, k_ref, v_ref, g_ref, gain_ref,
    x_st, y_st, r1, z_st, xr, w_st, yr, base, o_st, t_st, u_st, r2, xo,
    attn, s_hi, s_lo, p_hi, p_lo, a_hi, a_lo, qt, up, gk_loc, gv_loc,
    sq, cr, inv_b, coef_b, zbuf, gcore, gx, gy, gdp,
    y_in, z2_in, z4_in, in_sem, kv_sem, c1_s, c1_r, x1_s, x1_r, y_s, y_r, x2_s, x2_r, c2_s, c2_r,
    xo_s, xo_r, z_s, z_r, gc_s, gc_r, gx_s, gx_r, gy_s, gy_r, gd_s, gd_r,
):
    dp = lax.axis_index("dp")
    z = lax.axis_index("head")
    ctx = lax.axis_index("ctx")
    core = lax.rem(ctx, 2)
    x = lax.rem(ctx // 2, NX)
    y = ctx // (2 * NX)
    sx = jnp.where(core == 0, x, NX - 1 - x)
    sy = jnp.where(core == 0, y, NY - 1 - y)

    def at(yy, xx, cc):
        return {"ctx": (yy * NX + xx) * 2 + cc}

    sibling = at(y, x, 1 - core)
    xs = [lax.rem(x + d, NX) for d in (2, 1, 3)]
    ys = [lax.rem(y + d, NY) for d in range(1, NY)]
    zs = [lax.rem(z + d, NZ) for d in range(1, NZ)]

    def remote(src, dst, ssem, rsem, device):
        return pltpu.make_async_remote_copy(
            src_ref=src, dst_ref=dst, send_sem=ssem, recv_sem=rsem, device_id=device, device_id_type=MESH
        )

    def load(src, dst, sem):
        cp = pltpu.make_async_copy(src, dst, sem)
        cp.start()
        return cp

    def load_head(h):
        where = (slice(None), pl.ds(h * D, D))
        return [load(src.at[where], dst.at[where], kv_sem.at[i, h]) for i, (src, dst) in enumerate(((k_hbm, k_ref), (v_hbm, v_ref)))]

    kv_loads = [load_head(0)]
    bar = pltpu.get_barrier_semaphore()
    def tell(sem, device):
        pl.semaphore_signal(sem, inc=1, device_id=device, device_id_type=MESH)

    def z_at(d):
        return {"head": lax.rem(z + d + NZ, NZ)}

    peers = [at(y, v, c) for v in xs for c in (core, 1 - core)] + [at(v, x, core) for v in (ys[0], ys[2])]
    peers += [z_at(1), z_at(-1), {"dp": 1 - dp}, sibling]
    for p in peers:
        tell(bar, p)
    kv_loads += [load_head(h) for h in range(1, HEADS)]
    loads = [load(*c, in_sem.at[i]) for i, c in enumerate(((q_hbm, q_ref), (g_hbm, g_ref), (gain_hbm, gain_ref)))]

    flag = flag_ref[0]
    first0 = jnp.full((D, D), flag, jnp.int32) == 0
    low = jnp.full((D, D), core, jnp.int32) == 0
    causal = lax.broadcasted_iota(jnp.int32, (D, D), 0) >= lax.broadcasted_iota(jnp.int32, (D, D), 1)
    sends, late = [], []

    def drain(copies):
        for cp in copies:
            cp.wait_send()
        copies.clear()

    def drain_y(copies):
        for three in copies:
            for e, cp in enumerate(three, 1):

                @pl.when(sy + e < NY)
                def _():
                    cp.wait_send()

    def cols(h):
        return pl.ds(h * D, D)

    def rows(s):
        return pl.ds(s * D, D)

    def heads(chunk, body):
        for h in range(*chunk):
            body(h)

    def put_state(n, h, s0, s1, mask):
        first = jnp.where(mask, s0, s1)
        both = s0 + s1
        x_st[n, h] = jnp.where(low, first, both)
        y_st[n, h] = jnp.where(low, both, first)

    def stage_core(n, c):
        hs = pl.ds(CHUNKS[c][0], CHUNKS[c][1] - CHUNKS[c][0])
        here = pl.ds(pl.multiple_of(x * PART, PART), PART)
        if c in STRAIGHT:
            out = []
            for d, xx in enumerate(xs):
                there = pl.ds(pl.multiple_of(xx * PART, PART), PART)
                out.append(remote(x_st.at[n, hs, there], xr.at[n, sx, hs], x1_s.at[n, c, d], x1_r.at[n, c, d], at(y, xx, core)))
                out.append(remote(y_st.at[n, hs, there], xo.at[n, NX - 1 - sx], xo_s.at[n, d], xo_r.at[n, d], at(y, xx, 1 - core)))
            out.append(remote(y_st.at[n, hs, here], xo.at[n, NX - 1 - sx], xo_s.at[n, NX - 1], xo_r.at[n, NX - 1], sibling))
            for cp in out:
                cp.start()
            xr[n, sx, hs] = x_st[n, hs, here]
            sends.extend(out)
            return out
        cp = remote(y_st.at[n, hs], r1.at[n, hs], c1_s.at[n, c], c1_r.at[n, c], sibling)
        cp.start()
        sends.append(cp)
        return cp

    def stage_x(n, c, before):
        hs = pl.ds(CHUNKS[c][0], CHUNKS[c][1] - CHUNKS[c][0])
        if c in STRAIGHT:
            return before
        before.wait_recv()
        z_st[n, hs] = x_st[n, hs] + r1[n, hs]
        out = []
        for d, xx in enumerate(xs):
            there = pl.multiple_of(xx * PART, PART)
            cp = remote(
                z_st.at[n, hs, pl.ds(there, PART)], xr.at[n, sx, hs], x1_s.at[n, c, d], x1_r.at[n, c, d],
                at(y, xx, core),
            )
            cp.start()
            out.append(cp)
        xr[n, sx, hs] = z_st[n, hs, pl.ds(pl.multiple_of(x * PART, PART), PART)]
        sends.extend(out)
        return out

    def stage_y(n, c, before):
        hs = pl.ds(CHUNKS[c][0], CHUNKS[c][1] - CHUNKS[c][0])
        for cp in before:
            cp.wait_recv()
        if c in STRAIGHT:
            for t in range(NX):
                xr[n, t, hs] += xo[n, t]
        w_st[n, hs] = (xr[n, 0, hs] + xr[n, 1, hs]) + (xr[n, 2, hs] + xr[n, 3, hs])
        out = []
        for e in (2, 1, 3):
            yy = jnp.where(core == 0, lax.rem(y + e, NY), lax.rem(y + NY - e, NY))
            cp = remote(w_st.at[n, hs], yr.at[n, e - 1, hs], y_s.at[n, c, e - 1], y_r.at[n, c, e - 1], at(yy, x, core))

            @pl.when(sy + e < NY)
            def _():
                cp.start()

            out.append(cp)
        return [out[1], out[0], out[2]]

    def stage_back(n, c, before):
        hs = pl.ds(CHUNKS[c][0], CHUNKS[c][1] - CHUNKS[c][0])
        base[n, hs] = jnp.zeros_like(base[n, hs])
        for e, cp in enumerate(before, 1):

            @pl.when(sy >= e)
            def _():
                cp.wait_recv()
                base[n, hs] += yr[n, e - 1, hs]

        total = base[n, hs]
        for t in range(NX):
            o_st[n, t, hs] = total
            if t < NX - 1:
                total = total + xr[n, t, hs]
        out = []
        here = pl.ds(pl.multiple_of(x * PART, PART), PART)
        for d, xx in enumerate(xs):
            t = jnp.where(core == 0, xx, NX - 1 - xx)
            cp = remote(o_st.at[n, t, hs], t_st.at[n, hs, here], x2_s.at[n, c, d], x2_r.at[n, c, d], at(y, xx, core))
            cp.start()
            out.append(cp)
        t_st[n, hs, here] = o_st[n, sx, hs]
        sends.extend(out)
        return out

    def stage_swap(n, c, before):
        hs = pl.ds(CHUNKS[c][0], CHUNKS[c][1] - CHUNKS[c][0])
        for cp in before:
            cp.wait_recv()
        u_st[n, hs] = t_st[n, hs] + x_st[n, hs]
        cp = remote(u_st.at[n, hs], r2.at[n, hs], c2_s.at[n, c], c2_r.at[n, c], sibling)
        cp.start()
        late.append(cp)
        return cp

    def get_states(n, h, mask):
        mine, other = t_st[n, h], r2[n, h]
        own_first = jnp.where(low, x_st[n, h], y_st[n, h])
        first = jnp.where(low, mine, other)
        second = (mine + other) + own_first
        return jnp.where(mask, first, second), jnp.where(mask, second, first)

    c1 = []
    for c, chunk in enumerate(CHUNKS):

        def body(h):
            for cp in kv_loads[h]:
                cp.wait()
            kv = [mm(k_ref[rows(s), cols(h)], v_ref[rows(s), cols(h)], 0, 0) for s in range(2)]
            put_state(0, h, kv[0], kv[1], first0)

        heads(chunk, body)
        if c == 0:
            pl.semaphore_wait(bar, len(peers))
            tell(y_in, at(ys[0], x, core))
            tell(z2_in, z_at(1))
            tell(z2_in, z_at(-1))
        c1.append(stage_core(0, c))

    def local_attn(h):
        for s in range(2):
            qt[s, h] = jnp.transpose(q_ref[rows(s), cols(h)])
            up[s, h] = g_ref[rows(s), cols(h)].astype(F32) * gain[:, h * D : (h + 1) * D]
            scores = jnp.where(causal, mm(q_ref[rows(s), cols(h)], k_ref[rows(s), cols(h)], 1, 1), 0.0)
            hi, lo = parts(scores)
            s_hi[s, h] = hi
            s_lo[s, h] = lo
            vv = v_ref[rows(s), cols(h)]
            attn[s, h] = mm(wide(hi, lo), tall(vv, vv), 1, 0)

    x1 = [stage_x(0, c, c1[c]) for c in range(NC)]
    pl.semaphore_wait(y_in, 1)
    for cp in loads:
        cp.wait()
    gain = gain_ref[...].astype(F32).reshape(1, HEADS * D)
    heads((0, 2), local_attn)
    yy = [stage_y(0, c, x1[c]) for c in range(NC)]
    pl.semaphore_wait(z2_in, 2)
    tell(z4_in, z_at(2))
    tell(z4_in, z_at(2))
    tell(z4_in, z_at(-2))
    heads((2, 5), local_attn)
    x2 = [stage_back(0, c, yy[c]) for c in range(NC)]
    c2 = [stage_swap(0, c, x2[c]) for c in range(NC)]

    for c, chunk in enumerate(CHUNKS):
        c2[c].wait_recv()

        def body(h):
            prefix = get_states(0, h, first0)
            for s in range(2):
                hi, lo = parts(prefix[s])
                p_hi[s, h] = hi
                p_lo[s, h] = lo
                qq = q_ref[rows(s), cols(h)]
                a = attn[s, h] + mm(wide(qq, qq), tall(hi, lo), 1, 0)
                attn[s, h] = a
                if h == 0:
                    sq[s] = a * a
                    cr[s] = up[s, h] * a
                else:
                    sq[s] += a * a
                    cr[s] += up[s, h] * a

        heads(chunk, body)

    zero = jnp.zeros((8 - 4, D), F32)
    zbuf[z] = tall(*[jnp.sum(jnp.transpose(m), axis=0, keepdims=True) for m in (sq[0], sq[1], cr[0], cr[1])], zero)
    pl.semaphore_wait(z4_in, 3)
    zc = []
    for d, zz in enumerate(zs):
        cp = remote(zbuf.at[z], zbuf.at[z], z_s.at[d], z_r.at[d], {"head": zz})
        cp.start()
        zc.append(cp)
    drain(sends)
    drain(late)
    drain_y(yy)
    late.extend(zc)
    for cp in zc:
        cp.wait_recv()
    sums = zbuf[0]
    for i in range(1, NZ):
        sums = sums + zbuf[i]
    features = float(HEADS * D * NZ)
    inverse = lax.rsqrt(sums[0:2] * (1.0 / features) + 1e-6)
    coef = sums[2:4] * (inverse * inverse * inverse) * (1.0 / features)
    for s in range(2):
        inv_b[s] = jnp.transpose(jnp.broadcast_to(inverse[s : s + 1], (D, D)))
        coef_b[s] = jnp.transpose(jnp.broadcast_to(coef[s : s + 1], (D, D)))

    last0 = jnp.logical_not(first0)
    c1 = []
    for c, chunk in enumerate(CHUNKS):

        def body(h):
            adj = []
            for s in range(2):
                hi, lo = parts(up[s, h] * inv_b[s] - attn[s, h] * coef_b[s])
                a_hi[s, h] = hi
                a_lo[s, h] = lo
                qq = qt[s, h]
                adj.append(mm(wide(qq, qq), tall(hi, lo), 1, 0))
            put_state(1, h, adj[0], adj[1], last0)

        heads(chunk, body)
        c1.append(stage_core(1, c))

    def local_grads(h):
        for s in range(2):
            ah, al = a_hi[s, h], a_lo[s, h]
            sh, sl = s_hi[s, h], s_lo[s, h]
            ph, pw = p_hi[s, h], p_lo[s, h]
            qq, kk, vv = (r[rows(s), cols(h)] for r in (q_ref, k_ref, v_ref))
            gs = jnp.where(causal, mm(wide(ah, al), wide(vv, vv), 1, 1), 0.0)
            gh, gl = parts(gs)
            gq = mm(wide(gh, gl), tall(kk, kk), 1, 0) + mm(wide(ah, al, ah), wide(ph, ph, pw), 1, 1)
            oq_ref[rows(s), cols(h)] = gq.astype(BF16)
            gk_loc[s, h] = mm(tall(gh, gl), tall(qq, qq), 0, 0)
            gv_loc[s, h] = mm(tall(sh, sl, sh), tall(ah, ah, al), 0, 0)

    def gain_terms():
        out = []
        for h in range(HEADS):
            terms = [g_ref[rows(s), cols(h)].astype(F32) * attn[s, h] * inv_b[s] for s in range(2)]
            out.append(jnp.sum(terms[0] + terms[1], axis=0, keepdims=True))
        return tall(*out, jnp.zeros((8 - HEADS, D), F32))

    def gain_send(buf, me, ssem, rsem, devices):
        out = []
        for d, device in enumerate(devices):
            cp = remote(buf.at[me], buf.at[me], ssem.at[d], rsem.at[d], device)
            cp.start()
            out.append(cp)
        late.extend(out)
        return out

    def gain_sum(buf, count, copies):
        for cp in copies:
            cp.wait_recv()
        total = buf[0]
        for i in range(1, count):
            total = total + buf[i]
        return total

    x1 = [stage_x(1, c, c1[c]) for c in range(NC)]
    gcore[core] = gain_terms()
    gc = gain_send(gcore, core, gc_s, gc_r, [sibling])
    heads((0, 2), local_grads)
    yy = [stage_y(1, c, x1[c]) for c in range(NC)]
    gx[x] = gain_sum(gcore, 2, gc)
    gc = gain_send(gx, x, gx_s, gx_r, [at(y, v, core) for v in xs])
    heads((2, 4), local_grads)
    drain(sends)
    x2 = [stage_back(1, c, yy[c]) for c in range(NC)]
    gy[y] = gain_sum(gx, NX, gc)
    gc = gain_send(gy, y, gy_s, gy_r, [at(v, x, core) for v in ys])
    heads((4, 5), local_grads)
    drain_y(yy)
    c2 = [stage_swap(1, c, x2[c]) for c in range(NC)]
    drain(sends)
    gdp[dp] = gain_sum(gy, NY, gc)
    gc = gain_send(gdp, dp, gd_s, gd_r, [{"dp": 1 - dp}])

    for c, chunk in enumerate(CHUNKS):
        c2[c].wait_recv()

        def body(h):
            suffix = get_states(1, h, last0)
            for s in range(2):
                hi, lo = parts(suffix[s])
                kk, vv = (r[rows(s), cols(h)] for r in (k_ref, v_ref))
                gk = gk_loc[s, h] + mm(wide(vv, vv), wide(hi, lo), 1, 1)
                gv = gv_loc[s, h] + mm(wide(kk, kk), tall(hi, lo), 1, 0)
                ok_ref[rows(s), cols(h)] = gk.astype(BF16)
                ov_ref[rows(s), cols(h)] = gv.astype(BF16)

        heads(chunk, body)
    gg_ref[...] = gain_sum(gdp, 2, gc)

    drain(late)


def write_kernel(gq, gk, gv, gg, oq, ok, ov, og, sem):
    copies = []
    for i, (src, dst) in enumerate(((gq, oq), (gk, ok), (gv, ov))):
        for j in range(PIECES):
            rows = pl.ds(j * (src.shape[0] // PIECES), src.shape[0] // PIECES)
            copies.append(pltpu.make_async_copy(src.at[rows], dst.at[rows], sem.at[i, j]))
            copies[-1].start()
    for h in range(HEADS):
        og[pl.ds(h * D, D)] = gg[h]
    for cp in copies:
        cp.wait()


def shards(queries, keys, values, grad_out, gain, order_flag):
    shape = queries.shape
    tokens, width = shape[1], shape[2]
    flat = [a.reshape(tokens, width) for a in (queries, keys, values, grad_out)]
    gain = pltpu.with_memory_space_constraint(gain, pltpu.HBM)
    state = (2, HEADS, D, D)
    piece = (HEADS, PART, D)
    dma = pltpu.SemaphoreType.DMA
    scratch = [pltpu.VMEM((tokens, width), BF16)] * 4 + [pltpu.VMEM((width,), BF16)]
    scratch += [pltpu.VMEM(state, F32)] * 4
    scratch += [
        pltpu.VMEM((2, NX) + piece, F32),
        pltpu.VMEM((2,) + piece, F32),
        pltpu.VMEM((2, NY - 1) + piece, F32),
        pltpu.VMEM((2,) + piece, F32),
        pltpu.VMEM((2, NX) + piece, F32),
    ]
    scratch += [pltpu.VMEM(state, F32)] * 3
    scratch += [pltpu.VMEM((2, NX, 1, PART, D), F32)]
    scratch += [pltpu.VMEM(state, F32)]
    scratch += [pltpu.VMEM(state, BF16)] * 7
    scratch += [pltpu.VMEM(state, F32)] * 3
    scratch += [pltpu.VMEM((2, D, D), F32)] * 4
    scratch += [pltpu.VMEM((n, 8, D), F32) for n in (NZ, 2, NX, NY, 2)]
    scratch += [pltpu.SemaphoreType.REGULAR] * 3 + [dma((3,)), dma((2, HEADS))]
    for shape_of in ((2, NC), (2, NC, NX - 1), (2, NC, NY - 1), (2, NC, NX - 1), (2, NC)):
        scratch += [dma(shape_of)] * 2
    scratch += [dma((2, NX))] * 2
    for count in (NZ - 1, 1, NX - 1, NY - 1, 1):
        scratch += [dma((count,))] * 2
    hbm = pl.BlockSpec(memory_space=pl.ANY)
    vmem = pl.BlockSpec(memory_space=pltpu.VMEM)
    out = jax.ShapeDtypeStruct((tokens, width), BF16)
    inner = pltpu.VMEM((tokens, width), BF16)
    flat = [pltpu.with_memory_space_constraint(a, pltpu.HBM) for a in flat]
    gq, gk, gv, gg = pl.pallas_call(
        kernel,
        name="layer_backward",
        out_shape=(inner, inner, inner, jax.ShapeDtypeStruct((8, D), F32)),
        in_specs=[pl.BlockSpec(memory_space=pltpu.SMEM), hbm, hbm, hbm, hbm, hbm],
        out_specs=(vmem, vmem, vmem, vmem),
        scratch_shapes=scratch,
        compiler_params=pltpu.CompilerParams(
            collective_id=0, has_side_effects=True, vmem_limit_bytes=32 * 1024 * 1024
        ),
    )(order_flag, gain, *flat)
    gq, gk, gv = [pltpu.with_memory_space_constraint(a, pltpu.VMEM) for a in (gq, gk, gv)]
    gq, gk, gv, gg = pl.pallas_call(
        write_kernel,
        name="write_results",
        out_shape=(out, out, out, jax.ShapeDtypeStruct((width,), F32)),
        in_specs=[vmem, vmem, vmem, vmem],
        out_specs=(hbm, hbm, hbm, vmem),
        scratch_shapes=[dma((3, PIECES))],
        compiler_params=pltpu.CompilerParams(vmem_limit_bytes=32 * 1024 * 1024),
    )(gq, gk, gv, gg)
    return gq.reshape(shape), gk.reshape(shape), gv.reshape(shape), gg


def solution(mesh):
    rows = P("dp", "ctx", "head")
    return jax.shard_map(
        shards,
        mesh=mesh,
        in_specs=(rows, rows, rows, rows, P("head"), P("ctx")),
        out_specs=(rows, rows, rows, P("head")),
        check_vma=False,
    )
```

```python
import jax
import jax.numpy as jnp
from jax import lax
from jax.experimental import pallas as pl
from jax.experimental.pallas import tpu as pltpu
from jax.sharding import PartitionSpec as P

MESH = pl.DeviceIdType.MESH
D = 128
NX, NY, NZ = 4, 4, 8
HEADS = 5
PART = D // NX
CHUNKS = tuple((h, 0, PART) for h in range(HEADS))
NC = len(CHUNKS)
STRAIGHT = (0,)
F32, BF16 = jnp.float32, jnp.bfloat16


def mm(a, b, ca, cb):
    return lax.dot_general(a, b, (((ca,), (cb,)), ((), ())), preferred_element_type=F32)


def parts(x):
    hi = x.astype(BF16)
    return hi, (x - hi.astype(F32)).astype(BF16)


def wide(*a):
    return jnp.concatenate(a, axis=1)


def tall(*a):
    return jnp.concatenate(a, axis=0)


def kernel(
    flag_ref, gain_hbm, q_hbm, k_hbm, v_hbm, g_hbm,
    oq_ref, ok_ref, ov_ref, gg_ref,
    q_ref, k_ref, v_ref, g_ref, gain_ref,
    x_st, y_st, r1, z_st, xr, w_st, yr, o_st, t_st, u_st, r2, xo,
    attn, s_hi, s_lo, p_hi, p_lo, a_hi, a_lo, qt, up, gk_loc, gv_loc,
    sq, cr, inv_b, coef_b, zbuf, gcore, gx, gy, gdp,
    y_in, z2_in, z4_in, in_sem, kv_sem, c1_s, c1_r, x1_s, x1_r, y_s, y_r, x2_s, x2_r, c2_s, c2_r,
    xo_s, xo_r, z_s, z_r, gc_s, gc_r, gx_s, gx_r, gy_s, gy_r, gd_s, gd_r,
):
    dp = lax.axis_index("dp")
    z = lax.axis_index("head")
    ctx = lax.axis_index("ctx")
    core = lax.rem(ctx, 2)
    x = lax.rem(ctx // 2, NX)
    y = ctx // (2 * NX)
    sx = jnp.where(core == 0, x, NX - 1 - x)
    sy = jnp.where(core == 0, y, NY - 1 - y)

    def at(yy, xx, cc):
        return {"ctx": (yy * NX + xx) * 2 + cc}

    sibling = at(y, x, 1 - core)
    xs = [lax.rem(x + d, NX) for d in (2, 1, 3)]
    ys = [lax.rem(y + d, NY) for d in range(1, NY)]
    zs = [lax.rem(z + d, NZ) for d in range(1, NZ)]

    def remote(src, dst, ssem, rsem, device):
        return pltpu.make_async_remote_copy(
            src_ref=src, dst_ref=dst, send_sem=ssem, recv_sem=rsem, device_id=device, device_id_type=MESH
        )

    def load(src, dst, sem):
        cp = pltpu.make_async_copy(src, dst, sem)
        cp.start()
        return cp

    def load_head(h):
        where = (slice(None), pl.ds(h * D, D))
        return [load(src.at[where], dst.at[where], kv_sem.at[i, h]) for i, (src, dst) in enumerate(((k_hbm, k_ref), (v_hbm, v_ref)))]

    kv_loads = [load_head(0)]
    yr[...] = jnp.zeros_like(yr)
    bar = pltpu.get_barrier_semaphore()
    def tell(sem, device):
        pl.semaphore_signal(sem, inc=1, device_id=device, device_id_type=MESH)

    def z_at(d):
        return {"head": lax.rem(z + d + NZ, NZ)}

    peers = [at(y, v, c) for v in xs for c in (core, 1 - core)] + [at(v, x, core) for v in (ys[0], ys[2])]
    peers += [z_at(1), z_at(-1), {"dp": 1 - dp}, sibling]
    for p in peers:
        tell(bar, p)
    kv_loads += [load_head(h) for h in range(1, HEADS)]
    loads = [load(*c, in_sem.at[i]) for i, c in enumerate(((q_hbm, q_ref), (g_hbm, g_ref), (gain_hbm, gain_ref)))]

    flag = flag_ref[0]
    first0 = jnp.full((D, D), flag, jnp.int32) == 0
    low = jnp.full((D, D), core, jnp.int32) == 0
    causal = lax.broadcasted_iota(jnp.int32, (D, D), 0) >= lax.broadcasted_iota(jnp.int32, (D, D), 1)
    sends, late = [], []

    def drain(copies):
        for cp in copies:
            cp.wait_send()
        copies.clear()

    def drain_y(copies):
        for three in copies:
            for e, cp in enumerate(three, 1):

                @pl.when(sy + e < NY)
                def _():
                    cp.wait_send()

    def cols(h):
        return pl.ds(h * D, D)

    def rows(s):
        return pl.ds(s * D, D)

    def heads(chunk, body):
        for h in range(*chunk):
            body(h)

    def piece(c):
        h, r0, r1 = CHUNKS[c]
        return h, pl.ds(r0, r1 - r0)

    def put_state(n, h, s0, s1, mask):
        first = jnp.where(mask, s0, s1)
        both = s0 + s1
        x_st[n, h] = jnp.where(low, first, both).reshape(NX, PART, D)
        y_st[n, h] = jnp.where(low, both, first).reshape(NX, PART, D)

    def stage_core(n, c):
        h, rr = piece(c)
        if c in STRAIGHT:
            out = []
            for d, xx in enumerate(xs):
                out.append(remote(x_st.at[n, h, xx, rr], xr.at[n, sx, h, rr], x1_s.at[n, c, d], x1_r.at[n, c, d], at(y, xx, core)))
                out.append(remote(y_st.at[n, h, xx, rr], xo.at[n, NX - 1 - sx, rr], xo_s.at[n, c, d], xo_r.at[n, c, d], at(y, xx, 1 - core)))
            d = NX - 1
            out.append(remote(y_st.at[n, h, x, rr], xo.at[n, NX - 1 - sx, rr], xo_s.at[n, c, d], xo_r.at[n, c, d], sibling))
            for cp in out:
                cp.start()
            xr[n, sx, h, rr] = x_st[n, h, x, rr]
            sends.extend(out)
            return out
        cp = remote(y_st.at[n, h, :, rr], r1.at[n, h, :, rr], c1_s.at[n, c], c1_r.at[n, c], sibling)
        cp.start()
        sends.append(cp)
        return cp

    def stage_x(n, c, before):
        h, rr = piece(c)
        if c in STRAIGHT:
            return before
        before.wait_recv()
        z_st[n, h, :, rr] = x_st[n, h, :, rr] + r1[n, h, :, rr]
        out = []
        for d, xx in enumerate(xs):
            cp = remote(z_st.at[n, h, xx, rr], xr.at[n, sx, h, rr], x1_s.at[n, c, d], x1_r.at[n, c, d], at(y, xx, core))
            cp.start()
            out.append(cp)
        xr[n, sx, h, rr] = z_st[n, h, x, rr]
        sends.extend(out)
        return out

    def stage_y(n, c, before):
        h, rr = piece(c)
        for cp in before:
            cp.wait_recv()
        if c in STRAIGHT:
            for t in range(NX):
                xr[n, t, h, rr] += xo[n, t, rr]
        w_st[n, h, rr] = (xr[n, 0, h, rr] + xr[n, 1, h, rr]) + (xr[n, 2, h, rr] + xr[n, 3, h, rr])
        out = []
        for e in (2, 1, 3):
            yy = jnp.where(core == 0, lax.rem(y + e, NY), lax.rem(y + NY - e, NY))
            cp = remote(w_st.at[n, h, rr], yr.at[n, e - 1, h, rr], y_s.at[n, c, e - 1], y_r.at[n, c, e - 1], at(yy, x, core))

            @pl.when(sy + e < NY)
            def _():
                cp.start()

            out.append(cp)
        return [out[1], out[0], out[2]]

    def stage_back(n, c, before):
        h, rr = piece(c)
        for e, cp in enumerate(before, 1):
            pl.when(sy >= e)(cp.wait_recv)
        total = (yr[n, 0, h, rr] + yr[n, 1, h, rr]) + yr[n, 2, h, rr]
        for t in range(NX):
            o_st[n, t, h, rr] = total
            if t < NX - 1:
                total = total + xr[n, t, h, rr]
        out = []
        for d, xx in enumerate(xs):
            t = jnp.where(core == 0, xx, NX - 1 - xx)
            cp = remote(o_st.at[n, t, h, rr], t_st.at[n, h, x, rr], x2_s.at[n, c, d], x2_r.at[n, c, d], at(y, xx, core))
            cp.start()
            out.append(cp)
        t_st[n, h, x, rr] = o_st[n, sx, h, rr]
        sends.extend(out)
        return out

    def stage_swap(n, c, before):
        h, rr = piece(c)
        for cp in before:
            cp.wait_recv()
        u_st[n, h, :, rr] = t_st[n, h, :, rr] + x_st[n, h, :, rr]
        cp = remote(u_st.at[n, h, :, rr], r2.at[n, h, :, rr], c2_s.at[n, c], c2_r.at[n, c], sibling)
        cp.start()
        late.append(cp)
        return cp

    def get_states(n, h, mask):
        mine, other = t_st[n, h].reshape(D, D), r2[n, h].reshape(D, D)
        own_first = jnp.where(low, x_st[n, h].reshape(D, D), y_st[n, h].reshape(D, D))
        first = jnp.where(low, mine, other)
        second = (mine + other) + own_first
        return jnp.where(mask, first, second), jnp.where(mask, second, first)

    c1 = []
    for c, (h, r0, _) in enumerate(CHUNKS):
        if r0 == 0:
            for cp in kv_loads[h]:
                cp.wait()
            kv = [mm(k_ref[rows(s), cols(h)], v_ref[rows(s), cols(h)], 0, 0) for s in range(2)]
            put_state(0, h, kv[0], kv[1], first0)
        if c == 0:
            pl.semaphore_wait(bar, len(peers))
            tell(y_in, at(ys[0], x, core))
            tell(z2_in, z_at(1))
            tell(z2_in, z_at(-1))
        c1.append(stage_core(0, c))

    def local_attn(h):
        for s in range(2):
            qt[s, h] = jnp.transpose(q_ref[rows(s), cols(h)])
            up[s, h] = g_ref[rows(s), cols(h)].astype(F32) * gain[:, h * D : (h + 1) * D]
            scores = jnp.where(causal, mm(q_ref[rows(s), cols(h)], k_ref[rows(s), cols(h)], 1, 1), 0.0)
            hi, lo = parts(scores)
            s_hi[s, h] = hi
            s_lo[s, h] = lo
            vv = v_ref[rows(s), cols(h)]
            attn[s, h] = mm(wide(hi, lo), tall(vv, vv), 1, 0)

    x1 = [stage_x(0, c, c1[c]) for c in range(NC)]
    pl.semaphore_wait(y_in, 1)
    for cp in loads:
        cp.wait()
    gain = gain_ref[...].astype(F32).reshape(1, HEADS * D)
    heads((0, 2), local_attn)
    yy = [stage_y(0, c, x1[c]) for c in range(NC)]
    pl.semaphore_wait(z2_in, 2)
    tell(z4_in, z_at(2))
    tell(z4_in, z_at(2))
    tell(z4_in, z_at(-2))
    heads((2, 5), local_attn)
    x2 = [stage_back(0, c, yy[c]) for c in range(NC)]
    c2 = [stage_swap(0, c, x2[c]) for c in range(NC)]

    for h in range(HEADS):
        for c, chunk in enumerate(CHUNKS):
            if chunk[0] == h:
                c2[c].wait_recv()

        def body(h):
            prefix = get_states(0, h, first0)
            for s in range(2):
                hi, lo = parts(prefix[s])
                p_hi[s, h] = hi
                p_lo[s, h] = lo
                qq = q_ref[rows(s), cols(h)]
                a = attn[s, h] + mm(wide(qq, qq), tall(hi, lo), 1, 0)
                attn[s, h] = a
                if h == 0:
                    sq[s] = a * a
                    cr[s] = up[s, h] * a
                else:
                    sq[s] += a * a
                    cr[s] += up[s, h] * a

        body(h)

    zero = jnp.zeros((8 - 4, D), F32)
    zbuf[z] = tall(*[jnp.sum(jnp.transpose(m), axis=0, keepdims=True) for m in (sq[0], sq[1], cr[0], cr[1])], zero)
    pl.semaphore_wait(z4_in, 3)
    zc = []
    for d, zz in enumerate(zs):
        cp = remote(zbuf.at[z], zbuf.at[z], z_s.at[d], z_r.at[d], {"head": zz})
        cp.start()
        zc.append(cp)
    drain(sends)
    drain(late)
    drain_y(yy)
    sends.extend(zc)
    for cp in zc:
        cp.wait_recv()
    sums = zbuf[0]
    for i in range(1, NZ):
        sums = sums + zbuf[i]
    features = float(HEADS * D * NZ)
    inverse = lax.rsqrt(sums[0:2] * (1.0 / features) + 1e-6)
    coef = sums[2:4] * (inverse * inverse * inverse) * (1.0 / features)
    for s in range(2):
        inv_b[s] = jnp.transpose(jnp.broadcast_to(inverse[s : s + 1], (D, D)))
        coef_b[s] = jnp.transpose(jnp.broadcast_to(coef[s : s + 1], (D, D)))

    last0 = jnp.logical_not(first0)
    c1 = []
    for c, (h, r0, _) in enumerate(CHUNKS):

        def body(h):
            adj = []
            for s in range(2):
                hi, lo = parts(up[s, h] * inv_b[s] - attn[s, h] * coef_b[s])
                a_hi[s, h] = hi
                a_lo[s, h] = lo
                qq = qt[s, h]
                adj.append(mm(wide(qq, qq), tall(hi, lo), 1, 0))
            put_state(1, h, adj[0], adj[1], last0)

        if r0 == 0:
            body(h)
        c1.append(stage_core(1, c))

    def local_grads(h):
        for s in range(2):
            ah, al = a_hi[s, h], a_lo[s, h]
            sh, sl = s_hi[s, h], s_lo[s, h]
            ph, pw = p_hi[s, h], p_lo[s, h]
            qq, kk, vv = (r[rows(s), cols(h)] for r in (q_ref, k_ref, v_ref))
            gs = jnp.where(causal, mm(wide(ah, al), wide(vv, vv), 1, 1), 0.0)
            gh, gl = parts(gs)
            gq = mm(wide(gh, gl), tall(kk, kk), 1, 0) + mm(wide(ah, al, ah), wide(ph, ph, pw), 1, 1)
            oq_ref[rows(s), cols(h)] = gq.astype(BF16)
            gk_loc[s, h] = mm(tall(gh, gl), tall(qq, qq), 0, 0)
            gv_loc[s, h] = mm(tall(sh, sl, sh), tall(ah, ah, al), 0, 0)

    def gain_terms():
        out = []
        for h in range(HEADS):
            terms = [g_ref[rows(s), cols(h)].astype(F32) * attn[s, h] * inv_b[s] for s in range(2)]
            out.append(jnp.sum(terms[0] + terms[1], axis=0, keepdims=True))
        return tall(*out, jnp.zeros((8 - HEADS, D), F32))

    def gain_send(buf, me, ssem, rsem, devices):
        out = []
        for d, device in enumerate(devices):
            cp = remote(buf.at[me], buf.at[me], ssem.at[d], rsem.at[d], device)
            cp.start()
            out.append(cp)
        sends.extend(out)
        return out

    def gain_sum(buf, count, copies):
        for cp in copies:
            cp.wait_recv()
        total = buf[0]
        for i in range(1, count):
            total = total + buf[i]
        return total

    x1 = [stage_x(1, c, c1[c]) for c in range(NC)]
    gcore[core] = gain_terms()
    gc = gain_send(gcore, core, gc_s, gc_r, [sibling])
    heads((0, 2), local_grads)
    gx[x] = gain_sum(gcore, 2, gc)
    gc = gain_send(gx, x, gx_s, gx_r, [at(y, v, core) for v in xs])
    yy = [stage_y(1, c, x1[c]) for c in range(NC)]
    gy[y] = gain_sum(gx, NX, gc)
    gc = gain_send(gy, y, gy_s, gy_r, [at(v, x, core) for v in ys])
    heads((2, 4), local_grads)
    drain(sends)
    x2 = [stage_back(1, c, yy[c]) for c in range(NC)]
    gdp[dp] = gain_sum(gy, NY, gc)
    gc = gain_send(gdp, dp, gd_s, gd_r, [{"dp": 1 - dp}])
    heads((4, 5), local_grads)
    drain_y(yy)
    c2 = [stage_swap(1, c, x2[c]) for c in range(NC)]
    drain(sends)

    for h in range(HEADS):
        for c, chunk in enumerate(CHUNKS):
            if chunk[0] == h:
                c2[c].wait_recv()

        def body(h):
            suffix = get_states(1, h, last0)
            for s in range(2):
                hi, lo = parts(suffix[s])
                kk, vv = (r[rows(s), cols(h)] for r in (k_ref, v_ref))
                gk = gk_loc[s, h] + mm(wide(vv, vv), wide(hi, lo), 1, 1)
                gv = gv_loc[s, h] + mm(wide(kk, kk), tall(hi, lo), 1, 0)
                ok_ref[rows(s), cols(h)] = gk.astype(BF16)
                ov_ref[rows(s), cols(h)] = gv.astype(BF16)

        body(h)
    gg_ref[...] = gain_sum(gdp, 2, gc)

    drain(late)


def write_kernel(gq, gk, gv, gg, oq, ok, ov, og, line, sem):
    copies = [pltpu.make_async_copy(src, dst, sem.at[i]) for i, (src, dst) in enumerate(((gq, oq), (gk, ok), (gv, ov), (line, og)))]
    for cp in copies[:3]:
        cp.start()
    for h in range(HEADS):
        line[pl.ds(h * D, D)] = gg[h]
    copies[3].start()
    for cp in copies:
        cp.wait()


def shards(queries, keys, values, grad_out, gain, order_flag):
    shape = queries.shape
    tokens, width = shape[1], shape[2]
    flat = [a.reshape(tokens, width) for a in (queries, keys, values, grad_out)]
    gain = pltpu.with_memory_space_constraint(gain, pltpu.HBM)
    state = (2, HEADS, D, D)
    quarters = (2, HEADS, NX, PART, D)
    piece = (HEADS, PART, D)
    dma = pltpu.SemaphoreType.DMA
    scratch = [pltpu.VMEM((tokens, width), BF16)] * 4 + [pltpu.VMEM((width,), BF16)]
    scratch += [pltpu.VMEM(quarters, F32)] * 4
    scratch += [
        pltpu.VMEM((2, NX) + piece, F32),
        pltpu.VMEM((2,) + piece, F32),
        pltpu.VMEM((2, NY - 1) + piece, F32),
        pltpu.VMEM((2, NX) + piece, F32),
    ]
    scratch += [pltpu.VMEM(quarters, F32)] * 3
    scratch += [pltpu.VMEM((2, NX, PART, D), F32)]
    scratch += [pltpu.VMEM(state, F32)]
    scratch += [pltpu.VMEM(state, BF16)] * 7
    scratch += [pltpu.VMEM(state, F32)] * 3
    scratch += [pltpu.VMEM((2, D, D), F32)] * 4
    scratch += [pltpu.VMEM((n, 8, D), F32) for n in (NZ, 2, NX, NY, 2)]
    scratch += [pltpu.SemaphoreType.REGULAR] * 3 + [dma((3,)), dma((2, HEADS))]
    for shape_of in ((2, NC), (2, NC, NX - 1), (2, NC, NY - 1), (2, NC, NX - 1), (2, NC)):
        scratch += [dma(shape_of)] * 2
    scratch += [dma((2, len(STRAIGHT), NX))] * 2
    for count in (NZ - 1, 1, NX - 1, NY - 1, 1):
        scratch += [dma((count,))] * 2
    hbm = pl.BlockSpec(memory_space=pl.ANY)
    vmem = pl.BlockSpec(memory_space=pltpu.VMEM)
    out = jax.ShapeDtypeStruct((tokens, width), BF16)
    inner = pltpu.VMEM((tokens, width), BF16)
    flat = [pltpu.with_memory_space_constraint(a, pltpu.HBM) for a in flat]
    gq, gk, gv, gg = pl.pallas_call(
        kernel,
        name="layer_backward",
        out_shape=(inner, inner, inner, pltpu.VMEM((8, D), F32)),
        in_specs=[pl.BlockSpec(memory_space=pltpu.SMEM), hbm, hbm, hbm, hbm, hbm],
        out_specs=(vmem, vmem, vmem, vmem),
        scratch_shapes=scratch,
        compiler_params=pltpu.CompilerParams(
            collective_id=0, has_side_effects=True, vmem_limit_bytes=32 * 1024 * 1024
        ),
    )(order_flag, gain, *flat)
    results = [pltpu.with_memory_space_constraint(a, pltpu.VMEM) for a in (gq, gk, gv, gg)]
    gq, gk, gv, gg = pl.pallas_call(
        write_kernel,
        name="write_results",
        out_shape=(out, out, out, jax.ShapeDtypeStruct((width,), F32)),
        in_specs=[vmem, vmem, vmem, vmem],
        out_specs=(hbm, hbm, hbm, hbm),
        scratch_shapes=[pltpu.VMEM((width,), F32), dma((4,))],
        compiler_params=pltpu.CompilerParams(vmem_limit_bytes=32 * 1024 * 1024),
    )(*results)
    return gq.reshape(shape), gk.reshape(shape), gv.reshape(shape), gg


def solution(mesh):
    rows = P("dp", "ctx", "head")
    return jax.shard_map(
        shards,
        mesh=mesh,
        in_specs=(rows, rows, rows, rows, P("head"), P("ctx")),
        out_specs=(rows, rows, rows, P("head")),
        check_vma=False,
    )
```

```python
import jax
import jax.numpy as jnp
from jax import lax
from jax.experimental import pallas as pl
from jax.experimental.pallas import tpu as pltpu
from jax.sharding import PartitionSpec as P

MESH = pl.DeviceIdType.MESH
D = 128
NX, NY, NZ = 4, 4, 8
HEADS = 5
PART = D // NX
F32, BF16 = jnp.float32, jnp.bfloat16


def mm(a, b, ca, cb):
    return lax.dot_general(a, b, (((ca,), (cb,)), ((), ())), preferred_element_type=F32)


def parts(x):
    hi = x.astype(BF16)
    return hi, (x - hi.astype(F32)).astype(BF16)


def wide(*a):
    return jnp.concatenate(a, axis=1)


def tall(*a):
    return jnp.concatenate(a, axis=0)


def kernel(
    flag_ref, gain_hbm, q_hbm, k_hbm, v_hbm, g_hbm,
    oq_ref, ok_ref, ov_ref, gg_ref,
    q_ref, k_ref, v_ref, g_ref, gain_ref, gain_rows,
    x_st, y_st, r1, z_st, xr, w_st, yr, o_st, t_st, u_st, r2, xo,
    attn, s_hi, s_lo, p_hi, p_lo, a_hi, a_lo, qt, up, gk_loc, gv_loc,
    sq, cr, inv_b, coef_b, zbuf, gcore, gx, gy, gdp,
    y_in, z2_in, z4_in, in_sem, kv_sem, c1_s, c1_r, x1_s, x1_r, y_s, y_r, x2_s, x2_r, c2_s, c2_r,
    xo_s, xo_r, z_s, z_r, gc_s, gc_r, gx_s, gx_r, gy_s, gy_r, gd_s, gd_r,
):
    dp = lax.axis_index("dp")
    z = lax.axis_index("head")
    ctx = lax.axis_index("ctx")
    core = lax.rem(ctx, 2)
    x = lax.rem(ctx // 2, NX)
    y = ctx // (2 * NX)
    sx = jnp.where(core == 0, x, NX - 1 - x)
    sy = jnp.where(core == 0, y, NY - 1 - y)

    def at(yy, xx, cc):
        return {"ctx": (yy * NX + xx) * 2 + cc}

    sibling = at(y, x, 1 - core)
    xs = [lax.rem(x + d, NX) for d in (2, 1, 3)]
    ys = [lax.rem(y + d, NY) for d in range(1, NY)]
    zs = [lax.rem(z + d, NZ) for d in range(1, NZ)]
    bar = pltpu.get_barrier_semaphore()

    def remote(src, dst, ssem, rsem, device):
        return pltpu.make_async_remote_copy(
            src_ref=src, dst_ref=dst, send_sem=ssem, recv_sem=rsem, device_id=device, device_id_type=MESH
        )

    def start(copies):
        for cp in copies:
            cp.start()

    def received(copies):
        for cp in copies:
            cp.wait_recv()

    def sent(copies):
        for cp in copies:
            cp.wait_send()

    def loop(first, last, body):
        def step(h, carry):
            body(h)
            return carry

        lax.fori_loop(first, last, step, 0)

    def cols(h):
        return pl.ds(pl.multiple_of(h * D, D), D)

    def rows(s):
        return pl.ds(s * D, D)

    def tell(sem, device):
        pl.semaphore_signal(sem, inc=1, device_id=device, device_id_type=MESH)

    def z_at(d):
        return {"head": lax.rem(z + d + NZ, NZ)}

    def kv_loads(h):
        where = (slice(None), cols(h))
        pairs = ((k_hbm, k_ref), (v_hbm, v_ref))
        return [pltpu.make_async_copy(src.at[where], dst.at[where], kv_sem.at[i, h]) for i, (src, dst) in enumerate(pairs)]

    pairs = ((q_hbm, q_ref), (g_hbm, g_ref), (gain_hbm, gain_ref))
    loads = [pltpu.make_async_copy(src, dst, in_sem.at[i]) for i, (src, dst) in enumerate(pairs)]
    start(kv_loads(0))
    yr[...] = jnp.zeros_like(yr)
    peers = [at(y, v, c) for v in xs for c in (core, 1 - core)] + [at(v, x, core) for v in (ys[0], ys[2])]
    peers += [z_at(1), z_at(-1), {"dp": 1 - dp}, sibling]
    for p in peers:
        tell(bar, p)
    loop(1, HEADS, lambda h: start(kv_loads(h)))
    start(loads)

    first0 = jnp.full((D, D), flag_ref[0], jnp.int32) == 0
    last0 = jnp.logical_not(first0)
    low = jnp.full((D, D), core, jnp.int32) == 0
    causal = lax.broadcasted_iota(jnp.int32, (D, D), 0) >= lax.broadcasted_iota(jnp.int32, (D, D), 1)

    def core_copy(n, h):
        return remote(y_st.at[n, h], r1.at[n, h], c1_s.at[n, h], c1_r.at[n, h], sibling)

    def x_copies(n, h, src):
        return [
            remote(src.at[n, h, xx], xr.at[n, sx, h], x1_s.at[n, h], x1_r.at[n, h], at(y, xx, core))
            for xx in xs
        ]

    def straight_copies(n):
        to = [(xx, at(y, xx, 1 - core)) for xx in xs] + [(x, sibling)]
        return [
            remote(y_st.at[n, 0, xx], xo.at[n, NX - 1 - sx], xo_s.at[n], xo_r.at[n], device)
            for xx, device in to
        ]

    def y_copies(n, h):
        out = []
        for e in range(1, NY):
            yy = jnp.where(core == 0, lax.rem(y + e, NY), lax.rem(y + NY - e, NY))
            out.append(
                remote(w_st.at[n, h], yr.at[n, e - 1, h], y_s.at[n, h, e - 1], y_r.at[n, h, e - 1], at(yy, x, core))
            )
        return out

    def back_copies(n, h):
        out = []
        for xx in xs:
            t = jnp.where(core == 0, xx, NX - 1 - xx)
            out.append(remote(o_st.at[n, t, h], t_st.at[n, h, x], x2_s.at[n, h], x2_r.at[n, h], at(y, xx, core)))
        return out

    def x_all(n, h):
        three = xr.at[n, pl.ds(0, NX - 1), h]
        return remote(three, three, x1_s.at[n, h], x1_r.at[n, h], sibling)

    def straight_all(n):
        return remote(xo.at[n], xo.at[n], xo_s.at[n], xo_r.at[n], sibling)

    def back_all(n, h):
        three = t_st.at[n, h, pl.ds(0, NX - 1)]
        return remote(three, three, x2_s.at[n, h], x2_r.at[n, h], sibling)

    def swap_copy(n, h):
        return remote(u_st.at[n, h], r2.at[n, h], c2_s.at[n, h], c2_r.at[n, h], sibling)

    def put_state(n, h, s0, s1, mask):
        first = jnp.where(mask, s0, s1)
        both = s0 + s1
        x_st[n, h] = jnp.where(low, first, both).reshape(NX, PART, D)
        y_st[n, h] = jnp.where(low, both, first).reshape(NX, PART, D)

    def stage_straight(n):
        for a, b in zip(x_copies(n, 0, x_st), straight_copies(n)):
            a.start()
            b.start()
        straight_copies(n)[-1].start()
        xr[n, sx, 0] = x_st[n, 0, x]

    def stage_x(n, h):
        core_copy(n, h).wait_recv()
        z_st[n, h] = x_st[n, h] + r1[n, h]
        start(x_copies(n, h, z_st))
        xr[n, sx, h] = z_st[n, h, x]

    def stage_y(n, h):
        x_all(n, h).wait_recv()
        w_st[n, h] = (xr[n, 0, h] + xr[n, 1, h]) + (xr[n, 2, h] + xr[n, 3, h])
        copies = y_copies(n, h)
        for e in (2, 1, 3):
            pl.when(sy + e < NY)(copies[e - 1].start)

    def stage_y_straight(n):
        received([x_all(n, 0), straight_all(n)])
        total = None
        for t in range(NX):
            term = xr[n, t, 0] + xo[n, t]
            xr[n, t, 0] = term
            total = term if total is None else total + term
        w_st[n, 0] = total
        copies = y_copies(n, 0)
        for e in (2, 1, 3):
            pl.when(sy + e < NY)(copies[e - 1].start)

    def stage_back(n, h):
        for e, cp in enumerate(y_copies(n, h), 1):
            pl.when(sy >= e)(cp.wait_recv)
        total = (yr[n, 0, h] + yr[n, 1, h]) + yr[n, 2, h]
        for t in range(NX):
            o_st[n, t, h] = total
            if t < NX - 1:
                total = total + xr[n, t, h]
        start(back_copies(n, h))
        t_st[n, h, x] = o_st[n, sx, h]

    def stage_swap(n, h):
        back_all(n, h).wait_recv()
        u_st[n, h] = t_st[n, h] + x_st[n, h]
        swap_copy(n, h).start()

    def drain_first(n):
        sent([x_all(n, 0), straight_all(n)])

        def body(h):
            sent([core_copy(n, h), x_all(n, h)])

        loop(1, HEADS, body)

    def drain_y(n):
        def body(h):
            for e, cp in enumerate(y_copies(n, h), 1):
                pl.when(sy + e < NY)(cp.wait_send)

        loop(0, HEADS, body)

    def get_states(n, h, mask):
        swap_copy(n, h).wait_recv()
        mine, other = t_st[n, h].reshape(D, D), r2[n, h].reshape(D, D)
        own_first = jnp.where(low, x_st[n, h].reshape(D, D), y_st[n, h].reshape(D, D))
        first = jnp.where(low, mine, other)
        second = (mine + other) + own_first
        return jnp.where(mask, first, second), jnp.where(mask, second, first)

    def kv_state(h):
        for cp in kv_loads(h):
            cp.wait()
        kv = [mm(k_ref[rows(s), cols(h)], v_ref[rows(s), cols(h)], 0, 0) for s in range(2)]
        put_state(0, h, kv[0], kv[1], first0)

    kv_state(0)
    pl.semaphore_wait(bar, len(peers))
    stage_straight(0)
    tell(y_in, at(ys[0], x, core))
    tell(z2_in, z_at(1))
    tell(z2_in, z_at(-1))

    def next_kv(h):
        kv_state(h)
        core_copy(0, h).start()

    loop(1, HEADS, next_kv)
    loop(1, HEADS, lambda h: stage_x(0, h))
    for cp in loads:
        cp.wait()
    gain = gain_ref[...].astype(F32).reshape(1, HEADS * D)
    for h in range(HEADS):
        gain_rows[h : h + 1] = gain[:, h * D : (h + 1) * D]

    def local_attn(h):
        for s in range(2):
            qt[s, h] = jnp.transpose(q_ref[rows(s), cols(h)])
            up[s, h] = g_ref[rows(s), cols(h)].astype(F32) * gain_rows[pl.ds(h, 1)]
            scores = jnp.where(causal, mm(q_ref[rows(s), cols(h)], k_ref[rows(s), cols(h)], 1, 1), 0.0)
            hi, lo = parts(scores)
            s_hi[s, h] = hi
            s_lo[s, h] = lo
            vv = v_ref[rows(s), cols(h)]
            attn[s, h] = mm(wide(hi, lo), tall(vv, vv), 1, 0)

    pl.semaphore_wait(y_in, 1)
    stage_y_straight(0)
    local_attn(0)

    def next_y(h):
        stage_y(0, h)
        local_attn(h)

    loop(1, HEADS, next_y)
    pl.semaphore_wait(z2_in, 2)
    tell(z4_in, z_at(2))
    tell(z4_in, z_at(2))
    tell(z4_in, z_at(-2))
    sq[...] = jnp.zeros_like(sq)
    cr[...] = jnp.zeros_like(cr)
    loop(0, HEADS, lambda h: stage_back(0, h))
    loop(0, HEADS, lambda h: stage_swap(0, h))

    def full_attn(h):
        prefix = get_states(0, h, first0)
        for s in range(2):
            hi, lo = parts(prefix[s])
            p_hi[s, h] = hi
            p_lo[s, h] = lo
            qq = q_ref[rows(s), cols(h)]
            a = attn[s, h] + mm(wide(qq, qq), tall(hi, lo), 1, 0)
            attn[s, h] = a
            sq[s] += a * a
            cr[s] += up[s, h] * a

    loop(0, HEADS, full_attn)

    zero = jnp.zeros((8 - 4, D), F32)
    zbuf[z] = tall(*[jnp.sum(jnp.transpose(m), axis=0, keepdims=True) for m in (sq[0], sq[1], cr[0], cr[1])], zero)
    pl.semaphore_wait(z4_in, 3)
    start([remote(zbuf.at[z], zbuf.at[z], z_s, z_r, {"head": zz}) for zz in zs])
    seven = zbuf.at[pl.ds(0, NZ - 1)]
    z_all = remote(seven, seven, z_s, z_r, sibling)
    drain_first(0)
    drain_y(0)
    loop(0, HEADS, lambda h: sent([back_all(0, h), swap_copy(0, h)]))
    z_all.wait_recv()
    sums = zbuf[0]
    for i in range(1, NZ):
        sums = sums + zbuf[i]
    features = float(HEADS * D * NZ)
    inverse = lax.rsqrt(sums[0:2] * (1.0 / features) + 1e-6)
    coef = sums[2:4] * (inverse * inverse * inverse) * (1.0 / features)
    for s in range(2):
        inv_b[s] = jnp.transpose(jnp.broadcast_to(inverse[s : s + 1], (D, D)))
        coef_b[s] = jnp.transpose(jnp.broadcast_to(coef[s : s + 1], (D, D)))

    def adjoint(h):
        adj = []
        for s in range(2):
            hi, lo = parts(up[s, h] * inv_b[s] - attn[s, h] * coef_b[s])
            a_hi[s, h] = hi
            a_lo[s, h] = lo
            qq = qt[s, h]
            adj.append(mm(wide(qq, qq), tall(hi, lo), 1, 0))
        put_state(1, h, adj[0], adj[1], last0)

    adjoint(0)
    stage_straight(1)

    def next_adjoint(h):
        adjoint(h)
        core_copy(1, h).start()

    loop(1, HEADS, next_adjoint)

    def local_grads(h):
        for s in range(2):
            ah, al = a_hi[s, h], a_lo[s, h]
            sh, sl = s_hi[s, h], s_lo[s, h]
            ph, pw = p_hi[s, h], p_lo[s, h]
            qq, kk, vv = (r[rows(s), cols(h)] for r in (q_ref, k_ref, v_ref))
            gs = jnp.where(causal, mm(wide(ah, al), wide(vv, vv), 1, 1), 0.0)
            gh, gl = parts(gs)
            gq = mm(wide(gh, gl), tall(kk, kk), 1, 0) + mm(wide(ah, al, ah), wide(ph, ph, pw), 1, 1)
            oq_ref[rows(s), cols(h)] = gq.astype(BF16)
            gk_loc[s, h] = mm(tall(gh, gl), tall(qq, qq), 0, 0)
            gv_loc[s, h] = mm(tall(sh, sl, sh), tall(ah, ah, al), 0, 0)

    def gain_term(h):
        terms = [g_ref[rows(s), cols(h)].astype(F32) * attn[s, h] * inv_b[s] for s in range(2)]
        gcore[core, pl.ds(h, 1)] = jnp.sum(terms[0] + terms[1], axis=0, keepdims=True)

    def gain_send(buf, me, ssem, rsem, devices):
        copies = [remote(buf.at[me], buf.at[me], ssem.at[d], rsem.at[d], device) for d, device in enumerate(devices)]
        start(copies)
        return copies

    def gain_sum(buf, count, copies):
        received(copies)
        total = buf[0]
        for i in range(1, count):
            total = total + buf[i]
        return total

    loop(1, HEADS, lambda h: stage_x(1, h))
    gcore[core] = jnp.zeros((8, D), F32)
    loop(0, HEADS, gain_term)
    gain_1 = gain_send(gcore, core, gc_s, gc_r, [sibling])
    z_all.wait_send()
    stage_y_straight(1)
    local_grads(0)
    gx[x] = gain_sum(gcore, 2, gain_1)
    gain_2 = gain_send(gx, x, gx_s, gx_r, [at(y, v, core) for v in xs])

    def next_grads(h):
        stage_y(1, h)
        local_grads(h)

    loop(1, HEADS, next_grads)
    gy[y] = gain_sum(gx, NX, gain_2)
    gain_3 = gain_send(gy, y, gy_s, gy_r, [at(v, x, core) for v in ys])
    drain_first(1)
    loop(0, HEADS, lambda h: stage_back(1, h))
    gdp[dp] = gain_sum(gy, NY, gain_3)
    gain_4 = gain_send(gdp, dp, gd_s, gd_r, [{"dp": 1 - dp}])
    loop(0, HEADS, lambda h: stage_swap(1, h))
    drain_y(1)
    loop(0, HEADS, lambda h: back_all(1, h).wait_send())
    sent(gain_1 + gain_2 + gain_3 + gain_4)

    def last_grads(h):
        suffix = get_states(1, h, last0)
        for s in range(2):
            hi, lo = parts(suffix[s])
            kk, vv = (r[rows(s), cols(h)] for r in (k_ref, v_ref))
            gk = gk_loc[s, h] + mm(wide(vv, vv), wide(hi, lo), 1, 1)
            gv = gv_loc[s, h] + mm(wide(kk, kk), tall(hi, lo), 1, 0)
            ok_ref[rows(s), cols(h)] = gk.astype(BF16)
            ov_ref[rows(s), cols(h)] = gv.astype(BF16)

    loop(0, HEADS, last_grads)
    gg_ref[...] = gain_sum(gdp, 2, gain_4)
    loop(0, HEADS, lambda h: swap_copy(1, h).wait_send())


def write_kernel(gq, gk, gv, gg, oq, ok, ov, og, line, sem):
    copies = [pltpu.make_async_copy(src, dst, sem.at[i]) for i, (src, dst) in enumerate(((gq, oq), (gk, ok), (gv, ov), (line, og)))]
    for cp in copies[:3]:
        cp.start()
    for h in range(HEADS):
        line[pl.ds(h * D, D)] = gg[h]
    copies[3].start()
    for cp in copies:
        cp.wait()


def shards(queries, keys, values, grad_out, gain, order_flag):
    shape = queries.shape
    tokens, width = shape[1], shape[2]
    flat = [a.reshape(tokens, width) for a in (queries, keys, values, grad_out)]
    gain = pltpu.with_memory_space_constraint(gain, pltpu.HBM)
    state = (2, HEADS, D, D)
    quarters = (2, HEADS, NX, PART, D)
    piece = (HEADS, PART, D)
    dma = pltpu.SemaphoreType.DMA
    scratch = [pltpu.VMEM((tokens, width), BF16)] * 4 + [pltpu.VMEM((width,), BF16), pltpu.VMEM((8, D), F32)]
    scratch += [pltpu.VMEM(quarters, F32)] * 4
    scratch += [
        pltpu.VMEM((2, NX) + piece, F32),
        pltpu.VMEM((2,) + piece, F32),
        pltpu.VMEM((2, NY - 1) + piece, F32),
        pltpu.VMEM((2, NX) + piece, F32),
    ]
    scratch += [pltpu.VMEM(quarters, F32)] * 3
    scratch += [pltpu.VMEM((2, NX, PART, D), F32)]
    scratch += [pltpu.VMEM(state, F32)]
    scratch += [pltpu.VMEM(state, BF16)] * 7
    scratch += [pltpu.VMEM(state, F32)] * 3
    scratch += [pltpu.VMEM((2, D, D), F32)] * 4
    scratch += [pltpu.VMEM((n, 8, D), F32) for n in (NZ, 2, NX, NY, 2)]
    scratch += [pltpu.SemaphoreType.REGULAR] * 3 + [dma((3,)), dma((2, HEADS))]
    for shape_of in ((2, HEADS), (2, HEADS), (2, HEADS, NY - 1), (2, HEADS), (2, HEADS)):
        scratch += [dma(shape_of)] * 2
    scratch += [dma((2,))] * 2 + [dma] * 2
    for count in (1, NX - 1, NY - 1, 1):
        scratch += [dma((count,))] * 2
    hbm = pl.BlockSpec(memory_space=pl.ANY)
    vmem = pl.BlockSpec(memory_space=pltpu.VMEM)
    out = jax.ShapeDtypeStruct((tokens, width), BF16)
    inner = pltpu.VMEM((tokens, width), BF16)
    flat = [pltpu.with_memory_space_constraint(a, pltpu.HBM) for a in flat]
    gq, gk, gv, gg = pl.pallas_call(
        kernel,
        name="layer_backward",
        out_shape=(inner, inner, inner, pltpu.VMEM((8, D), F32)),
        in_specs=[pl.BlockSpec(memory_space=pltpu.SMEM), hbm, hbm, hbm, hbm, hbm],
        out_specs=(vmem, vmem, vmem, vmem),
        scratch_shapes=scratch,
        compiler_params=pltpu.CompilerParams(
            collective_id=0, has_side_effects=True, vmem_limit_bytes=32 * 1024 * 1024
        ),
    )(order_flag, gain, *flat)
    results = [pltpu.with_memory_space_constraint(a, pltpu.VMEM) for a in (gq, gk, gv, gg)]
    gq, gk, gv, gg = pl.pallas_call(
        write_kernel,
        name="write_results",
        out_shape=(out, out, out, jax.ShapeDtypeStruct((width,), F32)),
        in_specs=[vmem, vmem, vmem, vmem],
        out_specs=(hbm, hbm, hbm, hbm),
        scratch_shapes=[pltpu.VMEM((width,), F32), dma((4,))],
        compiler_params=pltpu.CompilerParams(vmem_limit_bytes=32 * 1024 * 1024),
    )(*results)
    return gq.reshape(shape), gk.reshape(shape), gv.reshape(shape), gg


def solution(mesh):
    rows = P("dp", "ctx", "head")
    return jax.shard_map(
        shards,
        mesh=mesh,
        in_specs=(rows, rows, rows, rows, P("head"), P("ctx")),
        out_specs=(rows, rows, rows, P("head")),
        check_vma=False,
    )
```

```python
import jax
import jax.numpy as jnp
from jax import lax
from jax.experimental import pallas as pl
from jax.experimental.pallas import tpu as pltpu
from jax.sharding import PartitionSpec as P

MESH = pl.DeviceIdType.MESH
D = 128
NX, NY, NZ = 4, 4, 8
HEADS = 5
PART = D // NX
F32, BF16 = jnp.float32, jnp.bfloat16


def mm(a, b, ca, cb):
    return lax.dot_general(a, b, (((ca,), (cb,)), ((), ())), preferred_element_type=F32)


def parts(x):
    hi = x.astype(BF16)
    return hi, (x - hi.astype(F32)).astype(BF16)


def wide(*a):
    return jnp.concatenate(a, axis=1)


def tall(*a):
    return jnp.concatenate(a, axis=0)


def kernel(
    flag_ref, gain_hbm, q_hbm, k_hbm, v_hbm, g_hbm,
    oq_ref, ok_ref, ov_ref, gg_ref,
    q_ref, k_ref, v_ref, g_ref, gain_ref, gain_rows,
    x_st, y_st, r1, z_st, xr, w_st, yr, o_st, t_st, u_st, r2, xo,
    attn, s_hi, s_lo, p_hi, p_lo, a_hi, a_lo, qt, up, gk_loc, gv_loc,
    sq, cr, inv_b, coef_b, zbuf, gcore, gx, gy, gdp,
    y_in, z2_in, z4_in, in_sem, kv_sem, c1_s, c1_r, x1_s, x1_r, y_s, y_r, x2_s, x2_r, c2_s, c2_r,
    xo_s, xo_r, z_s, z_r, gc_s, gc_r, gx_s, gx_r, gy_s, gy_r, gd_s, gd_r,
):
    dp = lax.axis_index("dp")
    z = lax.axis_index("head")
    ctx = lax.axis_index("ctx")
    core = lax.rem(ctx, 2)
    x = lax.rem(ctx // 2, NX)
    y = ctx // (2 * NX)
    sx = jnp.where(core == 0, x, NX - 1 - x)
    sy = jnp.where(core == 0, y, NY - 1 - y)

    def at(yy, xx, cc):
        return {"ctx": (yy * NX + xx) * 2 + cc}

    sibling = at(y, x, 1 - core)
    xs = [lax.rem(x + d, NX) for d in (2, 1, 3)]
    ys = [lax.rem(y + d, NY) for d in range(1, NY)]
    zs = [lax.rem(z + d, NZ) for d in range(1, NZ)]
    bar = pltpu.get_barrier_semaphore()

    def remote(src, dst, ssem, rsem, device):
        return pltpu.make_async_remote_copy(
            src_ref=src, dst_ref=dst, send_sem=ssem, recv_sem=rsem, device_id=device, device_id_type=MESH
        )

    def start(copies):
        for cp in copies:
            cp.start()

    def received(copies):
        for cp in copies:
            cp.wait_recv()

    def sent(copies):
        for cp in copies:
            cp.wait_send()

    def loop(first, last, body):
        def step(h, carry):
            body(h)
            return carry

        lax.fori_loop(first, last, step, 0)

    def cols(h):
        return pl.ds(pl.multiple_of(h * D, D), D)

    def rows(s):
        return pl.ds(s * D, D)

    def tell(sem, device):
        pl.semaphore_signal(sem, inc=1, device_id=device, device_id_type=MESH)

    def z_at(d):
        return {"head": lax.rem(z + d + NZ, NZ)}

    def kv_loads(h):
        where = (slice(None), cols(h))
        pairs = ((k_hbm, k_ref), (v_hbm, v_ref))
        return [pltpu.make_async_copy(src.at[where], dst.at[where], kv_sem.at[i, h]) for i, (src, dst) in enumerate(pairs)]

    pairs = ((q_hbm, q_ref), (g_hbm, g_ref), (gain_hbm, gain_ref))
    loads = [pltpu.make_async_copy(src, dst, in_sem.at[i]) for i, (src, dst) in enumerate(pairs)]
    start(kv_loads(0))
    yr[...] = jnp.zeros_like(yr)
    peers = [at(y, v, c) for v in xs for c in (core, 1 - core)] + [at(v, x, core) for v in (ys[0], ys[2])]
    peers += [z_at(1), z_at(-1), {"dp": 1 - dp}, sibling]
    for p in peers:
        tell(bar, p)
    loop(1, HEADS, lambda h: start(kv_loads(h)))
    start(loads)

    first0 = jnp.full((D, D), flag_ref[0], jnp.int32) == 0
    last0 = jnp.logical_not(first0)
    low = jnp.full((D, D), core, jnp.int32) == 0
    causal = lax.broadcasted_iota(jnp.int32, (D, D), 0) >= lax.broadcasted_iota(jnp.int32, (D, D), 1)

    def core_copy(n, h):
        return remote(y_st.at[n, h], r1.at[n, h], c1_s.at[n, h], c1_r.at[n, h], sibling)

    def x_copies(n, h, src):
        return [
            remote(src.at[n, h, xx], xr.at[n, sx, h], x1_s.at[n, h], x1_r.at[n, h], at(y, xx, core))
            for xx in xs
        ]

    def straight_copies(n):
        to = [(xx, at(y, xx, 1 - core)) for xx in xs] + [(x, sibling)]
        return [
            remote(y_st.at[n, 0, xx], xo.at[n, NX - 1 - sx], xo_s.at[n], xo_r.at[n], device)
            for xx, device in to
        ]

    def y_copies(n, h):
        out = []
        for e in range(1, NY):
            yy = jnp.where(core == 0, lax.rem(y + e, NY), lax.rem(y + NY - e, NY))
            out.append(
                remote(w_st.at[n, h], yr.at[n, e - 1, h], y_s.at[n, h], y_r.at[n, h], at(yy, x, core))
            )
        return out

    def back_copies(n, h):
        out = []
        for xx in xs:
            t = jnp.where(core == 0, xx, NX - 1 - xx)
            out.append(remote(o_st.at[n, t, h], t_st.at[n, h, x], x2_s.at[n, h], x2_r.at[n, h], at(y, xx, core)))
        return out

    def x_all(n, h):
        three = xr.at[n, pl.ds(0, NX - 1), h]
        return remote(three, three, x1_s.at[n, h], x1_r.at[n, h], sibling)

    def straight_all(n):
        return remote(xo.at[n], xo.at[n], xo_s.at[n], xo_r.at[n], sibling)

    def y_all(n, h, count):
        sums = yr.at[n, pl.ds(0, count), h]
        return remote(sums, sums, y_s.at[n, h], y_r.at[n, h], sibling)

    def back_all(n, h):
        three = t_st.at[n, h, pl.ds(0, NX - 1)]
        return remote(three, three, x2_s.at[n, h], x2_r.at[n, h], sibling)

    def swap_copy(n, h):
        return remote(u_st.at[n, h], r2.at[n, h], c2_s.at[n, h], c2_r.at[n, h], sibling)

    def put_state(n, h, s0, s1, mask):
        first = jnp.where(mask, s0, s1)
        both = s0 + s1
        x_st[n, h] = jnp.where(low, first, both).reshape(NX, PART, D)
        y_st[n, h] = jnp.where(low, both, first).reshape(NX, PART, D)

    def stage_straight(n):
        for a, b in zip(x_copies(n, 0, x_st), straight_copies(n)):
            a.start()
            b.start()
        straight_copies(n)[-1].start()
        xr[n, sx, 0] = x_st[n, 0, x]

    def stage_x(n, h):
        core_copy(n, h).wait_recv()
        z_st[n, h] = x_st[n, h] + r1[n, h]
        start(x_copies(n, h, z_st))
        xr[n, sx, h] = z_st[n, h, x]

    def stage_y(n, h):
        x_all(n, h).wait_recv()
        w_st[n, h] = (xr[n, 0, h] + xr[n, 1, h]) + (xr[n, 2, h] + xr[n, 3, h])
        copies = y_copies(n, h)
        for e in (2, 1, 3):
            pl.when(sy + e < NY)(copies[e - 1].start)

    def stage_y_straight(n):
        received([x_all(n, 0), straight_all(n)])
        total = None
        for t in range(NX):
            term = xr[n, t, 0] + xo[n, t]
            xr[n, t, 0] = term
            total = term if total is None else total + term
        w_st[n, 0] = total
        copies = y_copies(n, 0)
        for e in (2, 1, 3):
            pl.when(sy + e < NY)(copies[e - 1].start)

    def stage_back(n, h):
        for count in range(1, NY):
            pl.when(sy == count)(y_all(n, h, count).wait_recv)
        total = (yr[n, 0, h] + yr[n, 1, h]) + yr[n, 2, h]
        for t in range(NX):
            o_st[n, t, h] = total
            if t < NX - 1:
                total = total + xr[n, t, h]
        start(back_copies(n, h))
        t_st[n, h, x] = o_st[n, sx, h]

    def stage_swap(n, h):
        back_all(n, h).wait_recv()
        u_st[n, h] = t_st[n, h] + x_st[n, h]
        swap_copy(n, h).start()

    def drain_first(n):
        sent([x_all(n, 0), straight_all(n)])

        def body(h):
            sent([core_copy(n, h), x_all(n, h)])

        loop(1, HEADS, body)

    def drain_y(n):
        def body(h):
            for count in range(1, NY):
                pl.when(sy + count == NY - 1)(y_all(n, h, count).wait_send)

        loop(0, HEADS, body)

    def get_states(n, h, mask):
        swap_copy(n, h).wait_recv()
        mine, other = t_st[n, h].reshape(D, D), r2[n, h].reshape(D, D)
        own_first = jnp.where(low, x_st[n, h].reshape(D, D), y_st[n, h].reshape(D, D))
        first = jnp.where(low, mine, other)
        second = (mine + other) + own_first
        return jnp.where(mask, first, second), jnp.where(mask, second, first)

    def kv_state(h):
        for cp in kv_loads(h):
            cp.wait()
        kv = [mm(k_ref[rows(s), cols(h)], v_ref[rows(s), cols(h)], 0, 0) for s in range(2)]
        put_state(0, h, kv[0], kv[1], first0)

    kv_state(0)
    pl.semaphore_wait(bar, len(peers))
    stage_straight(0)
    tell(y_in, at(ys[0], x, core))
    tell(z2_in, z_at(1))
    tell(z2_in, z_at(-1))

    def next_kv(h):
        kv_state(h)
        core_copy(0, h).start()

    loop(1, HEADS, next_kv)
    loop(1, HEADS, lambda h: stage_x(0, h))
    for cp in loads:
        cp.wait()
    gain = gain_ref[...].astype(F32).reshape(1, HEADS * D)
    for h in range(HEADS):
        gain_rows[h : h + 1] = gain[:, h * D : (h + 1) * D]

    def local_attn(h):
        for s in range(2):
            qt[s, h] = jnp.transpose(q_ref[rows(s), cols(h)])
            up[s, h] = g_ref[rows(s), cols(h)].astype(F32) * gain_rows[pl.ds(h, 1)]
            scores = jnp.where(causal, mm(q_ref[rows(s), cols(h)], k_ref[rows(s), cols(h)], 1, 1), 0.0)
            hi, lo = parts(scores)
            s_hi[s, h] = hi
            s_lo[s, h] = lo
            vv = v_ref[rows(s), cols(h)]
            attn[s, h] = mm(wide(hi, lo), tall(vv, vv), 1, 0)

    pl.semaphore_wait(y_in, 1)
    stage_y_straight(0)
    local_attn(0)

    def next_y(h):
        stage_y(0, h)
        local_attn(h)

    loop(1, HEADS, next_y)
    pl.semaphore_wait(z2_in, 2)
    tell(z4_in, z_at(2))
    tell(z4_in, z_at(2))
    tell(z4_in, z_at(-2))
    sq[...] = jnp.zeros_like(sq)
    cr[...] = jnp.zeros_like(cr)
    loop(0, HEADS, lambda h: stage_back(0, h))
    loop(0, HEADS, lambda h: stage_swap(0, h))

    def full_attn(h):
        prefix = get_states(0, h, first0)
        for s in range(2):
            hi, lo = parts(prefix[s])
            p_hi[s, h] = hi
            p_lo[s, h] = lo
            qq = q_ref[rows(s), cols(h)]
            a = attn[s, h] + mm(wide(qq, qq), tall(hi, lo), 1, 0)
            attn[s, h] = a
            sq[s] += a * a
            cr[s] += up[s, h] * a

    loop(0, HEADS, full_attn)

    zero = jnp.zeros((8 - 4, D), F32)
    zbuf[z] = tall(*[jnp.sum(jnp.transpose(m), axis=0, keepdims=True) for m in (sq[0], sq[1], cr[0], cr[1])], zero)
    pl.semaphore_wait(z4_in, 3)
    start([remote(zbuf.at[z], zbuf.at[z], z_s, z_r, {"head": zz}) for zz in zs])
    seven = zbuf.at[pl.ds(0, NZ - 1)]
    z_all = remote(seven, seven, z_s, z_r, sibling)
    drain_first(0)
    drain_y(0)
    loop(0, HEADS, lambda h: sent([back_all(0, h), swap_copy(0, h)]))
    z_all.wait_recv()
    sums = zbuf[0]
    for i in range(1, NZ):
        sums = sums + zbuf[i]
    features = float(HEADS * D * NZ)
    inverse = lax.rsqrt(sums[0:2] * (1.0 / features) + 1e-6)
    coef = sums[2:4] * (inverse * inverse * inverse) * (1.0 / features)
    for s in range(2):
        inv_b[s] = jnp.transpose(jnp.broadcast_to(inverse[s : s + 1], (D, D)))
        coef_b[s] = jnp.transpose(jnp.broadcast_to(coef[s : s + 1], (D, D)))

    def adjoint(h):
        adj = []
        for s in range(2):
            hi, lo = parts(up[s, h] * inv_b[s] - attn[s, h] * coef_b[s])
            a_hi[s, h] = hi
            a_lo[s, h] = lo
            qq = qt[s, h]
            adj.append(mm(wide(qq, qq), tall(hi, lo), 1, 0))
        put_state(1, h, adj[0], adj[1], last0)

    adjoint(0)
    stage_straight(1)

    def next_adjoint(h):
        adjoint(h)
        core_copy(1, h).start()

    loop(1, HEADS, next_adjoint)

    def local_grads(h):
        for s in range(2):
            ah, al = a_hi[s, h], a_lo[s, h]
            sh, sl = s_hi[s, h], s_lo[s, h]
            ph, pw = p_hi[s, h], p_lo[s, h]
            qq, kk, vv = (r[rows(s), cols(h)] for r in (q_ref, k_ref, v_ref))
            gs = jnp.where(causal, mm(wide(ah, al), wide(vv, vv), 1, 1), 0.0)
            gh, gl = parts(gs)
            gq = mm(wide(gh, gl), tall(kk, kk), 1, 0) + mm(wide(ah, al, ah), wide(ph, ph, pw), 1, 1)
            oq_ref[rows(s), cols(h)] = gq.astype(BF16)
            gk_loc[s, h] = mm(tall(gh, gl), tall(qq, qq), 0, 0)
            gv_loc[s, h] = mm(tall(sh, sl, sh), tall(ah, ah, al), 0, 0)

    def gain_term(h):
        terms = [g_ref[rows(s), cols(h)].astype(F32) * attn[s, h] * inv_b[s] for s in range(2)]
        gcore[core, pl.ds(h, 1)] = jnp.sum(terms[0] + terms[1], axis=0, keepdims=True)

    def gain_send(buf, me, ssem, rsem, devices):
        start([remote(buf.at[me], buf.at[me], ssem, rsem, device) for device in devices])
        some = buf.at[pl.ds(0, len(devices))]
        return remote(some, some, ssem, rsem, sibling)

    def gain_sum(buf, count, copies):
        copies.wait_recv()
        total = buf[0]
        for i in range(1, count):
            total = total + buf[i]
        return total

    loop(1, HEADS, lambda h: stage_x(1, h))
    gcore[core] = jnp.zeros((8, D), F32)
    loop(0, HEADS, gain_term)
    gain_1 = gain_send(gcore, core, gc_s, gc_r, [sibling])
    z_all.wait_send()
    stage_y_straight(1)
    local_grads(0)
    gx[x] = gain_sum(gcore, 2, gain_1)
    gain_2 = gain_send(gx, x, gx_s, gx_r, [at(y, v, core) for v in xs])

    def next_grads(h):
        stage_y(1, h)
        local_grads(h)

    loop(1, HEADS, next_grads)
    gy[y] = gain_sum(gx, NX, gain_2)
    gain_3 = gain_send(gy, y, gy_s, gy_r, [at(v, x, core) for v in ys])
    drain_first(1)
    loop(0, HEADS, lambda h: stage_back(1, h))
    gdp[dp] = gain_sum(gy, NY, gain_3)
    gain_4 = gain_send(gdp, dp, gd_s, gd_r, [{"dp": 1 - dp}])
    loop(0, HEADS, lambda h: stage_swap(1, h))
    drain_y(1)
    loop(0, HEADS, lambda h: back_all(1, h).wait_send())
    sent([gain_1, gain_2, gain_3, gain_4])

    def last_grads(h):
        suffix = get_states(1, h, last0)
        for s in range(2):
            hi, lo = parts(suffix[s])
            kk, vv = (r[rows(s), cols(h)] for r in (k_ref, v_ref))
            gk = gk_loc[s, h] + mm(wide(vv, vv), wide(hi, lo), 1, 1)
            gv = gv_loc[s, h] + mm(wide(kk, kk), tall(hi, lo), 1, 0)
            ok_ref[rows(s), cols(h)] = gk.astype(BF16)
            ov_ref[rows(s), cols(h)] = gv.astype(BF16)

    loop(0, HEADS, last_grads)
    gg_ref[...] = gain_sum(gdp, 2, gain_4)
    loop(0, HEADS, lambda h: swap_copy(1, h).wait_send())


def write_kernel(gq, gk, gv, gg, oq, ok, ov, og, line, sem):
    copies = [pltpu.make_async_copy(src, dst, sem.at[i]) for i, (src, dst) in enumerate(((gq, oq), (gk, ok), (gv, ov), (line, og)))]
    for cp in copies[:3]:
        cp.start()
    for h in range(HEADS):
        line[pl.ds(h * D, D)] = gg[h]
    copies[3].start()
    for cp in copies:
        cp.wait()


def shards(queries, keys, values, grad_out, gain, order_flag):
    shape = queries.shape
    tokens, width = shape[1], shape[2]
    flat = [a.reshape(tokens, width) for a in (queries, keys, values, grad_out)]
    gain = pltpu.with_memory_space_constraint(gain, pltpu.HBM)
    state = (2, HEADS, D, D)
    quarters = (2, HEADS, NX, PART, D)
    piece = (HEADS, PART, D)
    dma = pltpu.SemaphoreType.DMA
    scratch = [pltpu.VMEM((tokens, width), BF16)] * 4 + [pltpu.VMEM((width,), BF16), pltpu.VMEM((8, D), F32)]
    scratch += [pltpu.VMEM(quarters, F32)] * 4
    scratch += [
        pltpu.VMEM((2, NX) + piece, F32),
        pltpu.VMEM((2,) + piece, F32),
        pltpu.VMEM((2, NY - 1) + piece, F32),
        pltpu.VMEM((2, NX) + piece, F32),
    ]
    scratch += [pltpu.VMEM(quarters, F32)] * 3
    scratch += [pltpu.VMEM((2, NX, PART, D), F32)]
    scratch += [pltpu.VMEM(state, F32)]
    scratch += [pltpu.VMEM(state, BF16)] * 7
    scratch += [pltpu.VMEM(state, F32)] * 3
    scratch += [pltpu.VMEM((2, D, D), F32)] * 4
    scratch += [pltpu.VMEM((n, 8, D), F32) for n in (NZ, 2, NX, NY, 2)]
    scratch += [pltpu.SemaphoreType.REGULAR] * 3 + [dma((3,)), dma((2, HEADS))]
    scratch += [dma((2, HEADS))] * 10
    scratch += [dma((2,))] * 2 + [dma] * 10
    hbm = pl.BlockSpec(memory_space=pl.ANY)
    vmem = pl.BlockSpec(memory_space=pltpu.VMEM)
    out = jax.ShapeDtypeStruct((tokens, width), BF16)
    inner = pltpu.VMEM((tokens, width), BF16)
    flat = [pltpu.with_memory_space_constraint(a, pltpu.HBM) for a in flat]
    gq, gk, gv, gg = pl.pallas_call(
        kernel,
        name="layer_backward",
        out_shape=(inner, inner, inner, pltpu.VMEM((8, D), F32)),
        in_specs=[pl.BlockSpec(memory_space=pltpu.SMEM), hbm, hbm, hbm, hbm, hbm],
        out_specs=(vmem, vmem, vmem, vmem),
        scratch_shapes=scratch,
        compiler_params=pltpu.CompilerParams(
            collective_id=0, has_side_effects=True, vmem_limit_bytes=32 * 1024 * 1024
        ),
    )(order_flag, gain, *flat)
    results = [pltpu.with_memory_space_constraint(a, pltpu.VMEM) for a in (gq, gk, gv, gg)]
    gq, gk, gv, gg = pl.pallas_call(
        write_kernel,
        name="write_results",
        out_shape=(out, out, out, jax.ShapeDtypeStruct((width,), F32)),
        in_specs=[vmem, vmem, vmem, vmem],
        out_specs=(hbm, hbm, hbm, hbm),
        scratch_shapes=[pltpu.VMEM((width,), F32), dma((4,))],
        compiler_params=pltpu.CompilerParams(vmem_limit_bytes=32 * 1024 * 1024),
    )(*results)
    return gq.reshape(shape), gk.reshape(shape), gv.reshape(shape), gg


def solution(mesh):
    rows = P("dp", "ctx", "head")
    return jax.shard_map(
        shards,
        mesh=mesh,
        in_specs=(rows, rows, rows, rows, P("head"), P("ctx")),
        out_specs=(rows, rows, rows, P("head")),
        check_vma=False,
    )
```
